128 devices in a mesh: ctx: 16 (over z, y_lo, core), tp: 8 (over y_hi, x).
Axes of the slice: x: 4, y: 4 (y_hi: 2, y_lo: 2; y = y_hi * 2 + y_lo), z: 4, core: 2. Of those that a mesh axis runs over, the one named last changes fastest.
Arguments:
- queries: bfloat16 [4096, 8192], P('ctx', 'tp'), may hold values from -5 to 5
- stretch_keys: bfloat16 [4096, 1024], P('ctx', 'tp'), may hold values from -5 to 5
- stretch_values: bfloat16 [4096, 1024], P('ctx', 'tp'), may hold values from -5 to 5
- cache_keys: bfloat16 [16384, 1024], P('ctx', 'tp'), may hold values from -5 to 5
- cache_values: bfloat16 [16384, 1024], P('ctx', 'tp'), may hold values from -5 to 5
- cached_len: int32 [1], replicated, may hold values from 8192 to 16384
- page_table: int32 [256], P('ctx'), may hold values from 0 to 255, as said below
- out_weight: bfloat16 [8192, 8192], P('tp', 'ctx'), may hold values from -1.5 to 1.5
Outputs:
- projected: bfloat16 [4096, 8192], P(('ctx', 'tp'))
- paged_kv: bfloat16 [256, 16, 2, 1024], P('ctx', None, None, 'tp')
The draws below stay inside these ranges and needn't reach their ends.
Inputs may be any that keep to these rules, and one draw needn't show every extreme that they name: Each destination page appears once; the pages of one index of ctx go to every instance page_table // 16 exactly 1 times.
All inputs are finite; a program needn't handle non-finite values.
Results may differ from the reference program's by a relative error of at most 0.02.
Values may be sent and summed in bfloat16 or wider, within the bound.
A program may use at most 128 MiB of HBM per device.

```python
import jax
import jax.numpy as jnp
from jax import lax

D = 8192
HEADS = 64
KV_HEADS = 8
D_HEAD = 128
PAGE = 16
TOKENS = 4096
CACHE = 16384
PAGES_DEV = 16
PAGES = 256
SENDS = 1
N_CTX = 16


def draw_queries(key, part):
    key = jax.random.fold_in(key, 5)
    values = jax.random.normal(key, (TOKENS, HEADS, D_HEAD), jnp.float32)
    return jnp.clip(values, -5.0, 5.0).reshape(TOKENS, HEADS * D_HEAD).astype(jnp.bfloat16)


def draw_cache_keys(key, part):
    key = jax.random.fold_in(key, 7)
    values = jax.random.normal(key, (CACHE, KV_HEADS, D_HEAD), jnp.float32)
    return jnp.clip(values, -5.0, 5.0).reshape(CACHE, KV_HEADS * D_HEAD).astype(jnp.bfloat16)


def draw_page_table(key, part):
    key = jax.random.fold_in(key, 11)
    first, second = jax.random.split(key)
    source_order = jax.vmap(lambda k: jax.random.permutation(k, PAGES_DEV))(jax.random.split(first, N_CTX))
    slot_order = jax.vmap(lambda k: jax.random.permutation(k, PAGES_DEV))(jax.random.split(second, N_CTX))
    pages = jnp.arange(PAGES, dtype=jnp.int32)
    owner = pages // PAGES_DEV
    within = pages % PAGES_DEV
    mixed = source_order[owner, within]
    target = mixed % N_CTX
    rank = owner * SENDS + mixed // N_CTX
    slot = slot_order[target, rank]
    return (target * PAGES_DEV + slot).astype(jnp.int32)


def levels(key, extent, pieces, smallest, largest):
    level = 1.0
    for position, parts in pieces:
        heights = jax.random.uniform(jax.random.fold_in(jax.random.fold_in(key, 6), position), (parts,), jnp.float32, smallest / len(pieces), largest / len(pieces))
        level = level * jnp.repeat(jnp.exp(heights), extent[position] // parts).reshape((-1,) + (1,) * (len(extent) - 1 - position))
    return level


def gaussian(rng, shape, scale, limit, cuts=(), kind=jnp.bfloat16):
    result = jax.random.normal(rng, shape, jnp.float32) * scale
    if len(cuts) > 0:
        result = levels(rng, shape, cuts, -0.22, 0.18) * result
    return jnp.clip(result, min=-limit, max=limit).astype(kind)


def setup_inputs(seed: int = 0) -> dict:
    streams_of = jax.random.split(jax.random.key(seed), 9)
    return {
        "queries": draw_queries(jax.random.fold_in(streams_of[8], 71), 0),
        "stretch_keys": gaussian(streams_of[1], (TOKENS, KV_HEADS * D_HEAD), 1.0, 5.0, ((0, 16), (1, 8))),
        "stretch_values": gaussian(streams_of[2], (TOKENS, KV_HEADS * D_HEAD), 1.0, 5.0, ((0, 16), (1, 8))),
        "cache_keys": draw_cache_keys(jax.random.fold_in(streams_of[8], 71), 0),
        "cache_values": gaussian(streams_of[4], (CACHE, KV_HEADS * D_HEAD), 1.0, 5.0, ((0, 16), (1, 8))),
        "cached_len": jax.random.randint(streams_of[5], (1,), CACHE // 2, CACHE + 1).astype(jnp.int32),
        "page_table": draw_page_table(jax.random.fold_in(streams_of[8], 71), 0),
        "out_weight": gaussian(streams_of[7], (HEADS * D_HEAD, D), (max(HEADS * D_HEAD // 512, 1)) ** -0.5, 1.5, ((0, 8), (1, 16))),
    }


def reference(queries, stretch_keys, stretch_values, cache_keys, cache_values, cached_len, page_table, out_weight):
    scale = D_HEAD ** -0.5
    length = cached_len[0]
    group = HEADS // KV_HEADS
    block = min(512, TOKENS)
    keys_all = jnp.concatenate([cache_keys, stretch_keys], axis=0)
    values_all = jnp.concatenate([cache_values, stretch_values], axis=0)
    positions = jnp.arange(CACHE + TOKENS, dtype=jnp.int32)

    def per_head(head):
        keys = lax.dynamic_slice_in_dim(keys_all, head * D_HEAD, D_HEAD, 1).astype(jnp.float32)
        values = lax.dynamic_slice_in_dim(values_all, head * D_HEAD, D_HEAD, 1).astype(jnp.float32)

        def per_block(index):
            rows = lax.dynamic_slice(queries, (index * block, head * group * D_HEAD), (block, group * D_HEAD))
            rows = rows.reshape(block, group, D_HEAD).astype(jnp.float32)
            scores = jnp.einsum("tjd,rd->jtr", rows, keys) * scale
            tokens = index * block + jnp.arange(block, dtype=jnp.int32)
            allowed = jnp.where(positions[None, :] < CACHE, positions[None, :] < length,
                                (positions[None, :] - CACHE) <= tokens[:, None])
            scores = jnp.where(allowed[None], scores, -jnp.inf)
            top = jnp.max(scores, axis=-1, keepdims=True)
            weights = jnp.where(allowed[None], jnp.exp(scores - top), 0.0)
            total = jnp.sum(weights, axis=-1)
            rounded = weights.astype(jnp.bfloat16).astype(jnp.float32)
            mixed = jnp.einsum("jtr,rd->jtd", rounded, values) / total[..., None]
            return jnp.transpose(mixed, (1, 0, 2)).reshape(block, group * D_HEAD).astype(jnp.bfloat16)

        return lax.map(per_block, jnp.arange(TOKENS // block)).reshape(TOKENS, group * D_HEAD)

    heads = lax.map(per_head, jnp.arange(KV_HEADS))
    attended = jnp.transpose(heads, (1, 0, 2)).reshape(TOKENS, HEADS * D_HEAD)
    projected = jnp.dot(attended, out_weight, preferred_element_type=jnp.float32).astype(jnp.bfloat16)
    pages = jnp.stack([stretch_keys, stretch_values], axis=1).reshape(PAGES, PAGE, 2, KV_HEADS * D_HEAD)
    paged_kv = jnp.zeros_like(pages).at[page_table].set(pages)
    return projected, paged_kv
```

```python
import functools
import math

import jax
import jax.numpy as jnp
from jax import lax
from jax.experimental import pallas as pl
from jax.experimental.pallas import tpu as pltpu
from jax.sharding import PartitionSpec as P

HEADS = 64
KV_HEADS = 8
D_HEAD = 128
PAGE = 16
GROUP = HEADS // KV_HEADS
ROWS = 256
QROWS = ROWS * GROUP
CSH = 1024
N_CTX = 16
N_TP = 8
UNIT = 1024
BASE = N_CTX * CSH
TILE = 1024
EXPC = D_HEAD ** (-0.5) * math.log2(math.e)
MIB = 2**20


class Place:
    def __init__(self):
        c = lax.axis_index("ctx")
        self.c = c
        self.z = c // 4
        self.y = lax.rem(c // 2, 2)
        self.core = lax.rem(c, 2)
        self.zp = lax.rem(c + 4, 16)
        self.zm = lax.rem(c + 12, 16)
        self.z2 = lax.rem(c + 8, 16)
        self.dy = 2 - 4 * self.y
        self.dm = 1 - 2 * self.core
        self.yp = c + self.dy
        self.mate = c + self.dm
        self.cy, self.zmy, self.zpy, self.z2y = (
            slot + self.dy for slot in (c, self.zm, self.zp, self.z2)
        )


class Flow:
    def __init__(self, place, view, send, recv, kind, halves=True):
        self.p, self.view, self.ss, self.rs = place, view, send, recv
        self.kind, self.halves = kind, halves
        self.sent = []

    def _copy(self, slot, part, dest, index):
        ref = self.view(slot, part)
        return pltpu.make_async_remote_copy(
            src_ref=ref,
            dst_ref=ref,
            send_sem=self.ss.at[index],
            recv_sem=self.rs.at[slot + (16 if part == 1 else 0)],
            device_id={"ctx": dest},
            device_id_type=pl.DeviceIdType.MESH,
        )

    def send(self, slot, part, dest):
        item = (slot, part, dest, len(self.sent))
        self.sent.append(item)
        self._copy(*item).start()

    def wait(self, slot, part=None):
        self._copy(slot, part, self.p.mate, 0).wait_recv()

    def finish(self):
        for item in self.sent:
            self._copy(*item).wait_send()

    def own(self):
        p = self.p
        if self.kind == "z":
            order = (p.zp, p.zm, p.yp, p.mate)
        else:
            order = (p.yp, p.zp, p.zm, p.mate)
        for dest in order:
            self.send(p.c, None, dest)

    def _down(self, slot):
        if self.kind == "z":
            self.send(slot, None, self.p.yp)
        self.send(slot, None, self.p.mate)

    def y(self, slot):
        self.wait(slot)
        if self.kind == "y":
            self.send(slot, None, self.p.zp)
            self.send(slot, None, self.p.zm)
        self.send(slot, None, self.p.mate)

    def from_zm(self, slot):
        self.wait(slot)
        self.send(slot, 0 if self.halves else None, self.p.zp)
        self._down(slot)

    def from_zp(self, slot):
        self.wait(slot)
        if self.halves:
            self.send(slot, 1, self.p.zm)
        self._down(slot)

    def from_z2(self, slot):
        if self.halves:
            self.wait(slot, 0)
            self.wait(slot, 1)
        else:
            self.wait(slot)
        self._down(slot)


def greet(partners):
    barrier = pltpu.get_barrier_semaphore()
    for partner in partners:
        pl.semaphore_signal(
            barrier, inc=1, device_id=partner, device_id_type=pl.DeviceIdType.MESH
        )
    pl.semaphore_wait(barrier, len(partners))


def attend(q, k, v, m_ref, l_ref, a_ref, rows, allowed=None):
    s = lax.dot_general(q, k, (((1,), (1,)), ((), ())), preferred_element_type=jnp.float32)
    if allowed is not None:
        s = jnp.where(allowed, s, -1e30)
    m = m_ref[rows, :]
    top = jnp.maximum(m, jnp.max(s, axis=1, keepdims=True))
    m_ref[rows, :] = top
    factor = jnp.exp2((m - top) * EXPC)
    w = jnp.exp2((s - jnp.tile(top, (1, s.shape[1] // 128))) * EXPC)
    l_ref[rows, :] = l_ref[rows, :] * factor + jnp.sum(w, axis=1, keepdims=True)
    a_ref[rows, :] = a_ref[rows, :] * factor + jnp.dot(
        w.astype(jnp.bfloat16), v, preferred_element_type=jnp.float32
    )


def gather_attend(
    q_ref, sk_ref, sv_ref, ck_ref, cv_ref, t_ref,
    m_ref, l_ref, a_ref, ko_ref, vo_ref, so_ref, to_ref,
    kbuf, vbuf, tbuf, qs, send, recv, tsend, trecv, local,
):
    p = Place()

    def cached(buf):
        def view(slot, part):
            rows = CSH if part is None else CSH // 2
            first = slot * CSH + (CSH // 2 if part == 1 else 0)
            return buf.at[pl.ds(pl.multiple_of(first, CSH // 2), rows)]
        return view

    def stretch(buf):
        def view(slot, part):
            rows = ROWS if part is None else ROWS // 2
            first = BASE + slot * ROWS + (ROWS // 2 if part == 1 else 0)
            return buf.at[pl.ds(pl.multiple_of(first, ROWS // 2), rows)]
        return view

    sk = Flow(p, stretch(kbuf), send.at[0], recv.at[0], "z")
    sv = Flow(p, stretch(vbuf), send.at[1], recv.at[1], "y")
    ck = Flow(p, cached(kbuf), send.at[2], recv.at[2], "z")
    cv = Flow(p, cached(vbuf), send.at[3], recv.at[3], "y")
    tb = Flow(p, lambda slot, part: tbuf.at[slot], tsend, trecv, "z", halves=False)

    own = [
        pltpu.make_async_copy(sk_ref, sk.view(p.c, None), local.at[0]),
        pltpu.make_async_copy(sv_ref, sv.view(p.c, None), local.at[1]),
        pltpu.make_async_copy(ck_ref, ck.view(p.c, None), local.at[2]),
        pltpu.make_async_copy(cv_ref, cv.view(p.c, None), local.at[3]),
    ]
    for copy in own:
        copy.start()
    tbuf[p.c] = t_ref[...]
    greet([{"ctx": x} for x in (p.zp, p.zm, p.yp, p.mate)])
    for copy, flow in zip(own, (sk, sv, ck, cv)):
        copy.wait()
        flow.own()
    tb.own()

    for h in range(GROUP):
        qs[pl.ds(h * ROWS, ROWS), :] = q_ref[:, pl.ds(h * D_HEAD, D_HEAD)]
    m_ref[...] = jnp.full_like(m_ref, -1e30)
    l_ref[...] = jnp.zeros_like(l_ref)
    a_ref[...] = jnp.zeros_like(a_ref)

    def mates(flow_k, flow_v, slot):
        flow_k.wait(slot)
        flow_v.wait(slot)

    def stretch_mates(group):
        for y in range(2):
            mates(sk, sv, group * 4 + y * 2 + 1 - p.core)

    sv.y(p.cy)
    sk.y(p.cy)
    stretch_mates(p.z)

    def near_stretch():
        sk.from_zm(p.zm)
        sk.from_zp(p.zp)
        sv.from_zm(p.zm)
        sv.from_zp(p.zp)
        sv.from_zm(p.zmy)
        sv.from_zp(p.zpy)
        tb.y(p.cy)
        tb.from_zm(p.zm)
        tb.from_zp(p.zp)

    def far_stretch():
        sk.y(p.zmy)
        sk.y(p.zpy)
        sk.from_z2(p.z2)
        sv.from_z2(p.z2)
        sv.from_z2(p.z2y)
        tb.y(p.zmy)
        tb.y(p.zpy)
        tb.from_z2(p.z2)

    def last_stretch():
        sk.y(p.z2y)
        tb.y(p.z2y)

    def own_cached():
        cv.y(p.cy)
        ck.y(p.cy)

    def near_cached_k():
        ck.from_zm(p.zm)
        ck.from_zp(p.zp)

    def near_cached_v():
        cv.from_zm(p.zm)
        cv.from_zp(p.zp)

    def near_cached_y():
        ck.y(p.zmy)
        ck.y(p.zpy)
        cv.from_zm(p.zmy)
        cv.from_zp(p.zpy)

    def far_cached():
        ck.from_z2(p.z2)
        cv.from_z2(p.z2)

    def far_cached_y():
        ck.y(p.z2y)
        cv.from_z2(p.z2y)

    outs = [
        pltpu.make_async_copy(kbuf.at[pl.ds(8 * CSH, 8 * CSH)], ko_ref, local.at[0]),
        pltpu.make_async_copy(vbuf.at[pl.ds(8 * CSH, 8 * CSH)], vo_ref, local.at[1]),
        pltpu.make_async_copy(kbuf.at[pl.ds(BASE, N_CTX * ROWS)], so_ref.at[0], local.at[2]),
        pltpu.make_async_copy(vbuf.at[pl.ds(BASE, N_CTX * ROWS)], so_ref.at[1], local.at[3]),
    ]

    def leftover():
        for slot in range(8, 16, 2):
            mates(ck, cv, slot + 1 - p.core)
        for group in range(4):
            @pl.when(group > p.z)
            def _():
                stretch_mates(group)
        for copy in outs:
            copy.start()

    events = {
        1: near_stretch,
        2: far_stretch,
        3: last_stretch,
        4: own_cached,
        5: near_cached_k,
        6: near_cached_v,
        8: near_cached_y,
        10: far_cached,
        12: far_cached_y,
        20: leftover,
    }

    def first_unit(r, carry):
        pl.when(r == 1)(events[1])
        rows = pl.ds(pl.multiple_of(r * TILE, TILE), TILE)
        keys = pl.ds(pl.multiple_of(BASE + p.z * UNIT, UNIT), UNIT)
        token = lax.broadcasted_iota(jnp.int32, (TILE, UNIT), 0) % ROWS
        place = lax.broadcasted_iota(jnp.int32, (TILE, UNIT), 1)
        allowed = place <= token + lax.rem(p.c, 4) * ROWS
        attend(qs[rows, :], kbuf[keys, :], vbuf[keys, :], m_ref, l_ref, a_ref, rows, allowed)
        return carry

    lax.fori_loop(0, 2, first_unit, 0)

    n_stretch = p.z + 1
    first = lax.rem((p.z + 1) // 2, 2)

    def later_unit(u, carry):
        for at, event in events.items():
            if at >= 2:
                pl.when(u == at)(event)
        i, r = u // 2, lax.rem(u, 2)
        is_stretch = i < n_stretch
        n = jnp.maximum(i - n_stretch, 0)
        group = jnp.where(n < 4, first, 1 - first)
        y = lax.rem(p.y + lax.rem(n, 4) // 2, 2)
        core = lax.rem(p.core + lax.rem(n, 2), 2)
        slot = group * 4 + y * 2 + core
        behind = jnp.maximum(p.z - i, 0)

        @pl.when(i < n_stretch + 8)
        def _():
            @pl.when((r == 0) & is_stretch)
            def _():
                stretch_mates(behind)

            @pl.when((r == 0) & jnp.logical_not(is_stretch) & (core != p.core))
            def _():
                mates(ck, cv, slot)

            start = jnp.where(is_stretch, BASE + behind * UNIT, slot * UNIT)
            keys = pl.ds(pl.multiple_of(start, UNIT), UNIT)
            rows = pl.ds(pl.multiple_of(r * TILE, TILE), TILE)
            attend(qs[rows, :], kbuf[keys, :], vbuf[keys, :], m_ref, l_ref, a_ref, rows)

        return carry

    lax.fori_loop(2, 24, later_unit, 0)

    for slot in range(0, 16, 2):
        tb.wait(slot + 1 - p.core)
    to_ref[...] = tbuf[...]
    for copy in outs:
        copy.wait()
    for flow in (sk, sv, ck, cv, tb):
        flow.finish()


def finish_attend(len_ref, q_ref, k_ref, v_ref, m_in, l_in, a_in, o_ref, m_ref, l_ref, a_ref, qs):
    for h in range(GROUP):
        qs[pl.ds(h * ROWS, ROWS), :] = q_ref[:, pl.ds(h * D_HEAD, D_HEAD)]
    m_ref[...] = m_in[...]
    l_ref[...] = l_in[...]
    a_ref[...] = a_in[...]
    more = len_ref[0] - 8 * CSH
    whole = more // UNIT

    def tile(r, keys, allowed):
        rows = pl.ds(pl.multiple_of(r * TILE, TILE), TILE)
        attend(qs[rows, :], k_ref[keys, :], v_ref[keys, :], m_ref, l_ref, a_ref, rows, allowed)

    def step(u, carry):
        tile(lax.rem(u, 2), pl.ds(pl.multiple_of(u // 2 * UNIT, UNIT), UNIT), None)
        return carry

    lax.fori_loop(0, whole * 2, step, 0)

    @pl.when(more - whole * UNIT > 0)
    def _():
        def part(r, carry):
            place = lax.broadcasted_iota(jnp.int32, (TILE, UNIT), 1)
            tile(r, pl.ds(pl.multiple_of(whole * UNIT, UNIT), UNIT), place < more - whole * UNIT)
            return carry

        lax.fori_loop(0, 2, part, 0)

    for h in range(GROUP):
        rows = pl.ds(h * ROWS, ROWS)
        o_ref[:, pl.ds(h * D_HEAD, D_HEAD)] = (a_ref[rows, :] / l_ref[rows, :]).astype(jnp.bfloat16)


def project(att_ref, w_ref, o_ref, x, w, yb, ob, asend, arecv, send, recv, osend, orecv, local):
    p = Place()
    t = lax.axis_index("tp")
    others = [lax.rem(t + d, N_TP) for d in range(1, N_TP)]
    ctx_others = [lax.rem(p.c + d, N_CTX) for d in range(1, N_CTX)]
    wcopy = pltpu.make_async_copy(w_ref, w, local.at[0])
    wcopy.start()

    def rows_of(s):
        return pl.ds(pl.multiple_of(s * 32, 32), 32)

    def cols_of(s, n):
        return pl.ds(pl.multiple_of(s * n, n), n)

    mine = pltpu.make_async_copy(att_ref.at[rows_of(t)], x.at[p.c, :, cols_of(t, 1024)], local.at[1])
    mine.start()
    greet([{"tp": s} for s in others] + [{"ctx": s} for s in ctx_others])

    def swap(source, dest, index):
        return pltpu.make_async_remote_copy(
            src_ref=att_ref.at[rows_of(dest)],
            dst_ref=x.at[p.c, :, cols_of(source, 1024)],
            send_sem=asend.at[index],
            recv_sem=arecv.at[source],
            device_id={"tp": dest},
            device_id_type=pl.DeviceIdType.MESH,
        )

    for index, s in enumerate(others):
        swap(t, s, index).start()
    mine.wait()
    for s in others:
        swap(s, s, 0).wait_recv()

    def halfrows(first):
        def view(slot, part):
            cols = pl.ds(0, 8192) if part is None else pl.ds(part * 4096, 4096)
            return x.at[slot, pl.ds(first, 16), cols]
        return view

    fz = Flow(p, halfrows(0), send.at[0], recv.at[0], "z")
    fy = Flow(p, halfrows(16), send.at[1], recv.at[1], "y")
    fy.own()
    fz.own()

    def give(dest, source, index):
        return pltpu.make_async_remote_copy(
            src_ref=yb.at[dest],
            dst_ref=ob.at[:, cols_of(source, 512)],
            send_sem=osend.at[index],
            recv_sem=orecv.at[source],
            device_id={"ctx": dest},
            device_id_type=pl.DeviceIdType.MESH,
        )

    def multiply(group):
        for y in range(2):
            for flow in (fz, fy):
                flow.wait(group * 4 + y * 2 + 1 - p.core)

        def part(k, total):
            cols = cols_of(k, 1024)
            a = x[pl.ds(group * 4, 4), :, cols].reshape(128, 1024)
            return total + jnp.dot(a, w[cols, :], preferred_element_type=jnp.float32)

        total = lax.fori_loop(0, 8, part, jnp.zeros((128, 512), jnp.float32))
        yb[pl.ds(group * 4, 4)] = total.astype(jnp.bfloat16).reshape(4, 32, 512)
        for j in range(4):
            dest = group * 4 + j

            @pl.when(dest != p.c)
            def _():
                give(dest, p.c, dest).start()

    fy.y(p.cy)
    fz.y(p.cy)
    fz.from_zm(p.zm)
    fz.from_zp(p.zp)
    fy.from_zm(p.zm)
    fy.from_zp(p.zp)
    wcopy.wait()
    multiply(p.z)
    ob[:, cols_of(p.c, 512)] = yb[p.c]
    fy.from_zm(p.zmy)
    fy.from_zp(p.zpy)
    fz.y(p.zmy)
    fz.y(p.zpy)
    fz.from_z2(p.z2)
    fy.from_z2(p.z2)
    multiply(p.zm // 4)
    fy.from_z2(p.z2y)
    fz.y(p.z2y)
    multiply(p.zp // 4)
    multiply(p.z2 // 4)

    for s in ctx_others:
        give(s, s, s).wait_recv()
    o_ref[...] = ob[...]
    for index, s in enumerate(others):
        swap(t, s, index).wait_send()
    for s in ctx_others:
        give(s, p.c, s).wait_send()
    fz.finish()
    fy.finish()


VMEM = pl.BlockSpec(memory_space=pltpu.VMEM)
ANY = pl.BlockSpec(memory_space=pl.ANY)


def local(
    queries,
    stretch_keys,
    stretch_values,
    cache_keys,
    cache_values,
    cached_len,
    page_table,
    out_weight,
):
    bf16, f32 = jnp.bfloat16, jnp.float32
    weight = lax.all_gather(out_weight, "tp", axis=0, tiled=True)
    table = jnp.broadcast_to(jnp.pad(page_table, (0, 112))[None], (8, 128))
    state = jax.ShapeDtypeStruct((QROWS, D_HEAD), f32)
    m, l, a, more_k, more_v, new, tables = pl.pallas_call(
        gather_attend,
        name="gather_attend",
        out_shape=(
            state,
            state,
            state,
            jax.ShapeDtypeStruct((8 * CSH, D_HEAD), bf16),
            jax.ShapeDtypeStruct((8 * CSH, D_HEAD), bf16),
            jax.ShapeDtypeStruct((2, N_CTX * ROWS, D_HEAD), bf16),
            jax.ShapeDtypeStruct((N_CTX, 8, 128), jnp.int32),
        ),
        in_specs=[VMEM, ANY, ANY, ANY, ANY, VMEM],
        out_specs=(VMEM, VMEM, VMEM, ANY, ANY, ANY, VMEM),
        scratch_shapes=[
            pltpu.VMEM((BASE + N_CTX * ROWS, D_HEAD), bf16),
            pltpu.VMEM((BASE + N_CTX * ROWS, D_HEAD), bf16),
            pltpu.VMEM((N_CTX, 8, 128), jnp.int32),
            pltpu.VMEM((QROWS, D_HEAD), bf16),
            pltpu.SemaphoreType.DMA((4, 20)),
            pltpu.SemaphoreType.DMA((4, 32)),
            pltpu.SemaphoreType.DMA((20,)),
            pltpu.SemaphoreType.DMA((32,)),
            pltpu.SemaphoreType.DMA((4,)),
        ],
        compiler_params=pltpu.CompilerParams(
            collective_id=1, has_side_effects=True, vmem_limit_bytes=52 * MIB
        ),
        cost_estimate=pl.CostEstimate(
            flops=4 * QROWS * 10 * UNIT * D_HEAD, bytes_accessed=20 * MIB, transcendentals=QROWS * 10 * UNIT
        ),
    )(queries, stretch_keys, stretch_values, cache_keys, cache_values, table)

    attended = pl.pallas_call(
        finish_attend,
        name="finish_attend",
        out_shape=jax.ShapeDtypeStruct((ROWS, GROUP * D_HEAD), bf16),
        in_specs=[pl.BlockSpec(memory_space=pltpu.SMEM)] + [VMEM] * 6,
        out_specs=VMEM,
        scratch_shapes=[
            pltpu.VMEM((QROWS, D_HEAD), f32),
            pltpu.VMEM((QROWS, D_HEAD), f32),
            pltpu.VMEM((QROWS, D_HEAD), f32),
            pltpu.VMEM((QROWS, D_HEAD), bf16),
        ],
        compiler_params=pltpu.CompilerParams(vmem_limit_bytes=52 * MIB),
        cost_estimate=pl.CostEstimate(
            flops=4 * QROWS * 4 * UNIT * D_HEAD, bytes_accessed=8 * MIB, transcendentals=QROWS * 4 * UNIT
        ),
    )(cached_len, queries, more_k, more_v, m, l, a)

    projected = pl.pallas_call(
        project,
        name="project",
        out_shape=jax.ShapeDtypeStruct((32, 8192), bf16),
        in_specs=[ANY, ANY],
        out_specs=VMEM,
        scratch_shapes=[
            pltpu.VMEM((N_CTX, 32, 8192), bf16),
            pltpu.VMEM((8192, 512), bf16),
            pltpu.VMEM((N_CTX, 32, 512), bf16),
            pltpu.VMEM((32, 8192), bf16),
            pltpu.SemaphoreType.DMA((N_TP,)),
            pltpu.SemaphoreType.DMA((N_TP,)),
            pltpu.SemaphoreType.DMA((2, 20)),
            pltpu.SemaphoreType.DMA((2, 32)),
            pltpu.SemaphoreType.DMA((N_CTX,)),
            pltpu.SemaphoreType.DMA((N_CTX,)),
            pltpu.SemaphoreType.DMA((2,)),
        ],
        compiler_params=pltpu.CompilerParams(
            collective_id=2, has_side_effects=True, vmem_limit_bytes=52 * MIB
        ),
        cost_estimate=pl.CostEstimate(
            flops=2 * 512 * 512 * 8192, bytes_accessed=20 * MIB, transcendentals=0
        ),
    )(attended, weight)

    all_table = tables[:, 0, :PAGE].reshape(-1)
    ctx_index = lax.axis_index("ctx")
    targets = ctx_index * 16 + jnp.arange(16, dtype=jnp.int32)
    matches = all_table[None, :] == targets[:, None]
    source = jnp.sum(
        jnp.where(matches, jnp.arange(all_table.shape[0], dtype=jnp.int32)[None, :], 0), axis=1
    )
    pages = new.reshape(2, 256, PAGE, D_HEAD)
    paged_kv = jnp.stack([pages[0][source], pages[1][source]], axis=2)
    return (projected, paged_kv)


def solution(mesh):
    return jax.shard_map(
        local,
        mesh=mesh,
        in_specs=(
            P("ctx", "tp"),
            P("ctx", "tp"),
            P("ctx", "tp"),
            P("ctx", "tp"),
            P("ctx", "tp"),
            P(),
            P("ctx"),
            P("tp", "ctx"),
        ),
        out_specs=(P(("ctx", "tp"), None), P("ctx", None, None, "tp")),
        check_vma=False,
    )
```

```python
import functools
import math

import jax
import jax.numpy as jnp
from jax import lax
from jax.experimental import pallas as pl
from jax.experimental.pallas import tpu as pltpu
from jax.sharding import PartitionSpec as P

HEADS = 64
KV_HEADS = 8
D_HEAD = 128
PAGE = 16
GROUP = HEADS // KV_HEADS
ROWS = 256
QROWS = ROWS * GROUP
CSH = 1024
N_CTX = 16
N_TP = 8
UNIT = 1024
BASE = N_CTX * CSH
TILE = 1024
EXPC = D_HEAD ** (-0.5) * math.log2(math.e)
MIB = 2**20


class Place:
    def __init__(self):
        c = lax.axis_index("ctx")
        self.c = c
        self.z = c // 4
        self.y = lax.rem(c // 2, 2)
        self.core = lax.rem(c, 2)
        self.zp = lax.rem(c + 4, 16)
        self.zm = lax.rem(c + 12, 16)
        self.z2 = lax.rem(c + 8, 16)
        self.dy = 2 - 4 * self.y
        self.dm = 1 - 2 * self.core
        self.yp = c + self.dy
        self.mate = c + self.dm
        self.cy, self.zmy, self.zpy, self.z2y = (
            slot + self.dy for slot in (c, self.zm, self.zp, self.z2)
        )


class Flow:
    def __init__(self, place, view, send, recv, kind, far="halves"):
        self.p, self.view, self.ss, self.rs = place, view, send, recv
        self.kind, self.far = kind, far
        self.sent = []

    def _copy(self, slot, part, dest, index):
        ref = self.view(slot, part)
        return pltpu.make_async_remote_copy(
            src_ref=ref,
            dst_ref=ref,
            send_sem=self.ss.at[index],
            recv_sem=self.rs.at[slot + (16 if part == 1 else 0)],
            device_id={"ctx": dest},
            device_id_type=pl.DeviceIdType.MESH,
        )

    def send(self, slot, part, dest):
        item = (slot, part, dest, len(self.sent))
        self.sent.append(item)
        self._copy(*item).start()

    def wait(self, slot, part=None):
        self._copy(slot, part, self.p.mate, 0).wait_recv()

    def finish(self):
        for item in self.sent:
            self._copy(*item).wait_send()

    def _along_z(self, slot):
        self.send(slot, None, self.p.zp)
        self.send(slot, None, self.p.zm)
        if self.far == "direct":
            self.send(slot, None, self.p.z2)

    def own(self):
        p = self.p
        if self.kind == "y":
            self.send(p.c, None, p.yp)
        self._along_z(p.c)
        if self.kind == "z":
            self.send(p.c, None, p.yp)
        self.send(p.c, None, p.mate)

    def _down(self, slot):
        if self.kind == "z":
            self.send(slot, None, self.p.yp)
        self.send(slot, None, self.p.mate)

    def y(self, slot):
        self.wait(slot)
        if self.kind == "y":
            self._along_z(slot)
        self.send(slot, None, self.p.mate)

    def from_zm(self, slot):
        self.wait(slot)
        if self.far == "halves":
            self.send(slot, 0, self.p.zp)
        self._down(slot)

    def from_zp(self, slot):
        self.wait(slot)
        if self.far == "halves":
            self.send(slot, 1, self.p.zm)
        self._down(slot)

    def from_z2(self, slot):
        if self.far == "halves":
            self.wait(slot, 0)
            self.wait(slot, 1)
        else:
            self.wait(slot)
        self._down(slot)


class Across:
    def __init__(self):
        t = lax.axis_index("tp")
        x = lax.rem(t, 4)
        self.t, self.x, self.h = t, x, t // 4
        self.rp, self.rm, self.r2 = (lax.rem(x + d, 4) for d in (1, 3, 2))
        self.xp, self.xm, self.x2 = (t - x + r for r in (self.rp, self.rm, self.r2))
        self.yh = lax.rem(t + 4, N_TP)


class Weight:
    def __init__(self, place, own, buf, send, recv):
        self.p, self.own, self.buf, self.ss, self.rs = place, own, buf, send, recv
        self.sent = []

    def _copy(self, src, slot, part, dest, index):
        rows = pl.ds(0, 1024) if part is None else pl.ds(part * 512, 512)
        dst = self.buf.at[slot, rows]
        return pltpu.make_async_remote_copy(
            src_ref=dst if src is None else src,
            dst_ref=dst,
            send_sem=self.ss.at[index],
            recv_sem=self.rs.at[slot + (4 if part == 1 else 0)],
            device_id={"tp": dest},
            device_id_type=pl.DeviceIdType.MESH,
        )

    def send(self, src, slot, part, dest):
        item = (src, slot, part, dest, len(self.sent))
        self.sent.append(item)
        self._copy(*item).start()

    def wait(self, slot, part=None):
        self._copy(None, slot, part, self.p.yh, 0).wait_recv()

    def start(self):
        self.send(self.own, self.p.x, None, self.p.xp)
        self.send(self.own, self.p.x, None, self.p.xm)

    def forward(self):
        self.wait(self.p.rm)
        self.send(None, self.p.rm, 0, self.p.xp)
        self.wait(self.p.rp)
        self.send(None, self.p.rp, 1, self.p.xm)

    def finish(self):
        self.wait(self.p.r2, 0)
        self.wait(self.p.r2, 1)
        for item in self.sent:
            self._copy(*item).wait_send()


def greet(partners):
    barrier = pltpu.get_barrier_semaphore()
    for partner in partners:
        pl.semaphore_signal(
            barrier, inc=1, device_id=partner, device_id_type=pl.DeviceIdType.MESH
        )
    pl.semaphore_wait(barrier, len(partners))


def attend(q, k, v, m_ref, l_ref, a_ref, rows, allowed=None):
    s = lax.dot_general(q, k, (((1,), (1,)), ((), ())), preferred_element_type=jnp.float32)
    if allowed is not None:
        s = jnp.where(allowed, s, -1e30)
    m = m_ref[rows, :]
    top = jnp.maximum(m, jnp.max(s, axis=1, keepdims=True))
    m_ref[rows, :] = top
    factor = jnp.exp2((m - top) * EXPC)
    w = jnp.exp2((s - jnp.tile(top, (1, s.shape[1] // 128))) * EXPC)
    l_ref[rows, :] = l_ref[rows, :] * factor + jnp.sum(w, axis=1, keepdims=True)
    a_ref[rows, :] = a_ref[rows, :] * factor + jnp.dot(
        w.astype(jnp.bfloat16), v, preferred_element_type=jnp.float32
    )


def gather_attend(
    q_ref, sk_ref, sv_ref, ck_ref, cv_ref, t_ref, w_ref,
    m_ref, l_ref, a_ref, ko_ref, vo_ref, so_ref, to_ref, wo_ref,
    kbuf, vbuf, tbuf, qs, send, recv, tsend, trecv, wsend, wrecv, local,
):
    p = Place()
    across = Across()
    wt = Weight(across, w_ref, wo_ref, wsend, wrecv)

    def cached(buf):
        def view(slot, part):
            rows = CSH if part is None else CSH // 2
            first = slot * CSH + (CSH // 2 if part == 1 else 0)
            return buf.at[pl.ds(pl.multiple_of(first, CSH // 2), rows)]
        return view

    def stretch(buf):
        def view(slot, part):
            rows = ROWS if part is None else ROWS // 2
            first = BASE + slot * ROWS + (ROWS // 2 if part == 1 else 0)
            return buf.at[pl.ds(pl.multiple_of(first, ROWS // 2), rows)]
        return view

    sk = Flow(p, stretch(kbuf), send.at[0], recv.at[0], "y", "direct")
    sv = Flow(p, stretch(vbuf), send.at[1], recv.at[1], "y", "direct")
    ck = Flow(p, cached(kbuf), send.at[2], recv.at[2], "z")
    cv = Flow(p, cached(vbuf), send.at[3], recv.at[3], "y")
    tb = Flow(p, lambda slot, part: tbuf.at[slot], tsend, trecv, "z", "direct")

    own = [
        pltpu.make_async_copy(sk_ref, sk.view(p.c, None), local.at[0]),
        pltpu.make_async_copy(sv_ref, sv.view(p.c, None), local.at[1]),
        pltpu.make_async_copy(ck_ref, ck.view(p.c, None), local.at[2]),
        pltpu.make_async_copy(cv_ref, cv.view(p.c, None), local.at[3]),
    ]
    for copy in own:
        copy.start()
    wown = pltpu.make_async_copy(w_ref, wo_ref.at[across.x], local.at[4])
    wown.start()
    tbuf[p.c] = t_ref[...]
    greet(
        [{"ctx": x} for x in (p.zp, p.zm, p.z2, p.yp, p.mate)]
        + [{"tp": x} for x in (across.xp, across.xm)]
    )
    own[0].wait()
    own[1].wait()
    sv.own()
    sk.own()
    tb.own()
    wt.start()

    for h in range(GROUP):
        qs[pl.ds(h * ROWS, ROWS), :] = q_ref[:, pl.ds(h * D_HEAD, D_HEAD)]
    m_ref[...] = jnp.full_like(m_ref, -1e30)
    l_ref[...] = jnp.zeros_like(l_ref)
    a_ref[...] = jnp.zeros_like(a_ref)

    def mates(flow_k, flow_v, slot):
        flow_k.wait(slot)
        flow_v.wait(slot)

    def stretch_mates(group):
        for y in range(2):
            mates(sk, sv, group * 4 + y * 2 + 1 - p.core)

    sv.y(p.cy)
    sk.y(p.cy)
    own[2].wait()
    own[3].wait()
    ck.own()
    cv.own()
    stretch_mates(p.z)

    def near_stretch():
        for flow in (sk, sv):
            flow.from_zm(p.zm)
            flow.from_zp(p.zp)

    def near_stretch_y():
        for flow in (sk, sv):
            flow.from_zm(p.zmy)
            flow.from_zp(p.zpy)

    def far_stretch():
        for flow in (sk, sv):
            flow.from_z2(p.z2)
            flow.from_z2(p.z2y)

    def tables():
        tb.y(p.cy)
        for slot in (p.zm, p.zp, p.z2):
            tb.from_z2(slot)

    def tables_y():
        for slot in (p.zmy, p.zpy, p.z2y):
            tb.y(slot)

    def near_cached_k():
        ck.from_zm(p.zm)
        ck.from_zp(p.zp)

    def own_cached():
        cv.y(p.cy)
        ck.y(p.cy)

    def near_cached_v():
        cv.from_zm(p.zm)
        cv.from_zp(p.zp)

    def near_cached_y():
        ck.from_z2(p.z2)
        ck.y(p.zmy)
        ck.y(p.zpy)
        cv.from_zm(p.zmy)
        cv.from_zp(p.zpy)
        cv.from_z2(p.z2)

    def far_cached():
        ck.y(p.z2y)
        cv.from_z2(p.z2y)

    outs = [
        pltpu.make_async_copy(kbuf.at[pl.ds(8 * CSH, 8 * CSH)], ko_ref, local.at[0]),
        pltpu.make_async_copy(vbuf.at[pl.ds(8 * CSH, 8 * CSH)], vo_ref, local.at[1]),
        pltpu.make_async_copy(kbuf.at[pl.ds(BASE, N_CTX * ROWS)], so_ref.at[0], local.at[2]),
        pltpu.make_async_copy(vbuf.at[pl.ds(BASE, N_CTX * ROWS)], so_ref.at[1], local.at[3]),
    ]

    def leftover():
        for slot in range(8, 16, 2):
            mates(ck, cv, slot + 1 - p.core)
        for group in range(4):
            @pl.when(group > p.z)
            def _():
                stretch_mates(group)
        for copy in outs:
            copy.start()

    events = {
        1: near_stretch,
        2: near_stretch_y,
        3: far_stretch,
        5: own_cached,
        6: near_cached_k,
        8: near_cached_v,
        9: wt.forward,
        11: near_cached_y,
        14: far_cached,
        16: tables,
        18: tables_y,
        20: leftover,
    }

    def first_unit(r, carry):
        pl.when(r == 1)(events[1])
        rows = pl.ds(pl.multiple_of(r * TILE, TILE), TILE)
        keys = pl.ds(pl.multiple_of(BASE + p.z * UNIT, UNIT), UNIT)
        token = lax.broadcasted_iota(jnp.int32, (TILE, UNIT), 0) % ROWS
        place = lax.broadcasted_iota(jnp.int32, (TILE, UNIT), 1)
        allowed = place <= token + lax.rem(p.c, 4) * ROWS
        attend(qs[rows, :], kbuf[keys, :], vbuf[keys, :], m_ref, l_ref, a_ref, rows, allowed)
        return carry

    lax.fori_loop(0, 2, first_unit, 0)

    n_stretch = p.z + 1
    first = lax.rem((p.z + 1) // 2, 2)
    c_start = 2 + 2 * (p.z // 2)

    def later_unit(u, carry):
        for at, event in events.items():
            if at >= 2:
                pl.when(u == at)(event)
        i, r = u // 2, lax.rem(u, 2)
        is_stretch = i < n_stretch
        n = jnp.maximum(i - c_start, 0)
        group = jnp.where(n < 4, first, 1 - first)
        y = lax.rem(p.y + lax.rem(n, 4) // 2, 2)
        core = lax.rem(p.core + lax.rem(n, 2), 2)
        slot = group * 4 + y * 2 + core
        behind = jnp.maximum(p.z - i, 0)

        @pl.when(is_stretch | ((i >= c_start) & (i < c_start + 8)))
        def _():
            @pl.when((r == 0) & is_stretch)
            def _():
                stretch_mates(behind)

            @pl.when((r == 0) & jnp.logical_not(is_stretch) & (core != p.core))
            def _():
                mates(ck, cv, slot)

            start = jnp.where(is_stretch, BASE + behind * UNIT, slot * UNIT)
            keys = pl.ds(pl.multiple_of(start, UNIT), UNIT)
            rows = pl.ds(pl.multiple_of(r * TILE, TILE), TILE)
            attend(qs[rows, :], kbuf[keys, :], vbuf[keys, :], m_ref, l_ref, a_ref, rows)

        return carry

    lax.fori_loop(2, 24, later_unit, 0)

    for slot in range(0, 16, 2):
        tb.wait(slot + 1 - p.core)
    to_ref[...] = tbuf[...]
    for copy in outs:
        copy.wait()
    wown.wait()
    for flow in (sk, sv, ck, cv, tb, wt):
        flow.finish()


def finish_attend(len_ref, q_ref, k_ref, v_ref, m_in, l_in, a_in, o_ref, m_ref, l_ref, a_ref, qs):
    for h in range(GROUP):
        qs[pl.ds(h * ROWS, ROWS), :] = q_ref[:, pl.ds(h * D_HEAD, D_HEAD)]
    m_ref[...] = m_in[...]
    l_ref[...] = l_in[...]
    a_ref[...] = a_in[...]
    more = len_ref[0] - 8 * CSH
    whole = more // UNIT

    def tile(r, keys, allowed):
        rows = pl.ds(pl.multiple_of(r * TILE, TILE), TILE)
        attend(qs[rows, :], k_ref[keys, :], v_ref[keys, :], m_ref, l_ref, a_ref, rows, allowed)

    def step(u, carry):
        tile(lax.rem(u, 2), pl.ds(pl.multiple_of(u // 2 * UNIT, UNIT), UNIT), None)
        return carry

    lax.fori_loop(0, whole * 2, step, 0)

    @pl.when(more - whole * UNIT > 0)
    def _():
        def part(r, carry):
            place = lax.broadcasted_iota(jnp.int32, (TILE, UNIT), 1)
            tile(r, pl.ds(pl.multiple_of(whole * UNIT, UNIT), UNIT), place < more - whole * UNIT)
            return carry

        lax.fori_loop(0, 2, part, 0)

    for h in range(GROUP):
        rows = pl.ds(h * ROWS, ROWS)
        o_ref[:, pl.ds(h * D_HEAD, D_HEAD)] = (a_ref[rows, :] / l_ref[rows, :]).astype(jnp.bfloat16)


def project(
    att_ref, w_ref, o_ref,
    x, w, pb, qb, keep, yb, ob,
    asend, arecv, send, recv, psend, precv, osend, orecv, local,
):
    p = Place()
    ac = Across()
    x_others = ((ac.rp, ac.xp), (ac.rm, ac.xm), (ac.r2, ac.x2))
    ctx_others = [lax.rem(p.c + d, N_CTX) for d in range(1, N_CTX)]
    wcopy = pltpu.make_async_copy(w_ref, w, local.at[0])
    wcopy.start()

    def rows_of(r, j):
        return pl.ds(pl.multiple_of((r + 4 * j) * 32, 32), 32)

    def cols_of(s, n):
        return pl.ds(pl.multiple_of(s * n, n), n)

    mine = [
        pltpu.make_async_copy(
            att_ref.at[rows_of(ac.x, j)], x.at[p.c, j, :, cols_of(ac.x, 1024)], local.at[1 + j]
        )
        for j in range(2)
    ]
    for copy in mine:
        copy.start()
    greet([{"tp": s} for s in (ac.xp, ac.xm, ac.x2, ac.yh)] + [{"ctx": s} for s in ctx_others])

    def swap(j, r, dest, source, index):
        return pltpu.make_async_remote_copy(
            src_ref=att_ref.at[rows_of(r, j)],
            dst_ref=x.at[p.c, j, :, cols_of(source, 1024)],
            send_sem=asend.at[j, index],
            recv_sem=arecv.at[j, source],
            device_id={"tp": dest},
            device_id_type=pl.DeviceIdType.MESH,
        )

    for j in (1, 0):
        for index, (r, dest) in enumerate(x_others):
            swap(j, r, dest, ac.x, index).start()

    def half(j):
        def view(slot, part):
            cols = pl.ds(0, 4096) if part is None else pl.ds(part * 2048, 2048)
            return x.at[slot, j, :, cols]
        return view

    fz = Flow(p, half(0), send.at[0], recv.at[0], "z")
    fy = Flow(p, half(1), send.at[1], recv.at[1], "y")
    for j, flow in ((1, fy), (0, fz)):
        mine[j].wait()
        for r, dest in x_others:
            swap(j, r, dest, r, 0).wait_recv()
        flow.own()

    def give(dest, source, index):
        return pltpu.make_async_remote_copy(
            src_ref=yb.at[dest],
            dst_ref=ob.at[:, cols_of(source, 512)],
            send_sem=osend.at[index],
            recv_sem=orecv.at[source],
            device_id={"ctx": dest},
            device_id_type=pl.DeviceIdType.MESH,
        )

    def cross(group):
        slots = pl.ds(group * 4, 4)
        return pltpu.make_async_remote_copy(
            src_ref=pb.at[slots],
            dst_ref=qb.at[slots],
            send_sem=psend.at[group],
            recv_sem=precv.at[group],
            device_id={"tp": ac.yh},
            device_id_type=pl.DeviceIdType.MESH,
        )

    def multiply(group):
        slots = pl.ds(group * 4, 4)
        for y in range(2):
            for flow in (fz, fy):
                flow.wait(group * 4 + y * 2 + 1 - p.core)

        def part(j):
            def step(k, total):
                a = x[slots, j, :, cols_of(k, 1024)].reshape(128, 1024)
                return total + jnp.dot(a, w[k], preferred_element_type=jnp.float32)

            return lax.fori_loop(0, 4, step, jnp.zeros((128, 512), jnp.float32)).reshape(4, 32, 512)

        pb[slots] = part(1 - ac.h).astype(jnp.bfloat16)
        cross(group).start()
        keep[slots] = part(ac.h)

    def combine(group):
        slots = pl.ds(group * 4, 4)
        cross(group).wait_recv()
        yb[slots] = (keep[slots] + qb[slots].astype(jnp.float32)).astype(jnp.bfloat16)
        for i in range(4):
            dest = group * 4 + i

            @pl.when(dest != p.c)
            def _():
                give(dest, p.c, dest).start()

    g0, gm, gp, g2 = p.z, p.zm // 4, p.zp // 4, p.z2 // 4
    fy.y(p.cy)
    fz.y(p.cy)
    fz.from_zm(p.zm)
    fz.from_zp(p.zp)
    fy.from_zm(p.zm)
    fy.from_zp(p.zp)
    wcopy.wait()
    multiply(g0)
    fy.from_zm(p.zmy)
    fy.from_zp(p.zpy)
    fz.y(p.zmy)
    fz.y(p.zpy)
    fz.from_z2(p.z2)
    fy.from_z2(p.z2)
    combine(g0)
    ob[:, cols_of(p.c, 512)] = yb[p.c]
    multiply(gm)
    fy.from_z2(p.z2y)
    fz.y(p.z2y)
    multiply(gp)
    combine(gm)
    multiply(g2)
    combine(gp)
    combine(g2)

    for s in ctx_others:
        give(s, s, s).wait_recv()
    o_ref[...] = ob[...]
    for j in range(2):
        for index, (r, dest) in enumerate(x_others):
            swap(j, r, dest, ac.x, index).wait_send()
    for s in ctx_others:
        give(s, p.c, s).wait_send()
    for group in range(4):
        cross(group).wait_send()
    for flow in (fz, fy):
        flow.finish()


VMEM = pl.BlockSpec(memory_space=pltpu.VMEM)
ANY = pl.BlockSpec(memory_space=pl.ANY)


def local(
    queries,
    stretch_keys,
    stretch_values,
    cache_keys,
    cache_values,
    cached_len,
    page_table,
    out_weight,
):
    bf16, f32 = jnp.bfloat16, jnp.float32
    table = jnp.broadcast_to(jnp.pad(page_table, (0, 112))[None], (8, 128))
    state = jax.ShapeDtypeStruct((QROWS, D_HEAD), f32)
    m, l, a, more_k, more_v, new, tables, weight = pl.pallas_call(
        gather_attend,
        name="gather_attend",
        out_shape=(
            state,
            state,
            state,
            jax.ShapeDtypeStruct((8 * CSH, D_HEAD), bf16),
            jax.ShapeDtypeStruct((8 * CSH, D_HEAD), bf16),
            jax.ShapeDtypeStruct((2, N_CTX * ROWS, D_HEAD), bf16),
            jax.ShapeDtypeStruct((N_CTX, 8, 128), jnp.int32),
            jax.ShapeDtypeStruct((4, 1024, 512), bf16),
        ),
        in_specs=[VMEM, ANY, ANY, ANY, ANY, VMEM, ANY],
        out_specs=(VMEM, VMEM, VMEM, ANY, ANY, ANY, VMEM, ANY),
        scratch_shapes=[
            pltpu.VMEM((BASE + N_CTX * ROWS, D_HEAD), bf16),
            pltpu.VMEM((BASE + N_CTX * ROWS, D_HEAD), bf16),
            pltpu.VMEM((N_CTX, 8, 128), jnp.int32),
            pltpu.VMEM((QROWS, D_HEAD), bf16),
            pltpu.SemaphoreType.DMA((4, 20)),
            pltpu.SemaphoreType.DMA((4, 32)),
            pltpu.SemaphoreType.DMA((20,)),
            pltpu.SemaphoreType.DMA((32,)),
            pltpu.SemaphoreType.DMA((8,)),
            pltpu.SemaphoreType.DMA((N_TP,)),
            pltpu.SemaphoreType.DMA((5,)),
        ],
        compiler_params=pltpu.CompilerParams(
            collective_id=1, has_side_effects=True, vmem_limit_bytes=62 * MIB
        ),
        cost_estimate=pl.CostEstimate(
            flops=4 * QROWS * 10 * UNIT * D_HEAD, bytes_accessed=20 * MIB, transcendentals=QROWS * 10 * UNIT
        ),
    )(queries, stretch_keys, stretch_values, cache_keys, cache_values, table, out_weight)

    attended = pl.pallas_call(
        finish_attend,
        name="finish_attend",
        out_shape=jax.ShapeDtypeStruct((ROWS, GROUP * D_HEAD), bf16),
        in_specs=[pl.BlockSpec(memory_space=pltpu.SMEM)] + [VMEM] * 6,
        out_specs=VMEM,
        scratch_shapes=[
            pltpu.VMEM((QROWS, D_HEAD), f32),
            pltpu.VMEM((QROWS, D_HEAD), f32),
            pltpu.VMEM((QROWS, D_HEAD), f32),
            pltpu.VMEM((QROWS, D_HEAD), bf16),
        ],
        compiler_params=pltpu.CompilerParams(vmem_limit_bytes=62 * MIB),
        cost_estimate=pl.CostEstimate(
            flops=4 * QROWS * 4 * UNIT * D_HEAD, bytes_accessed=8 * MIB, transcendentals=QROWS * 4 * UNIT
        ),
    )(cached_len, queries, more_k, more_v, m, l, a)

    projected = pl.pallas_call(
        project,
        name="project",
        out_shape=jax.ShapeDtypeStruct((32, 8192), bf16),
        in_specs=[ANY, ANY],
        out_specs=VMEM,
        scratch_shapes=[
            pltpu.VMEM((N_CTX, 2, 32, 4096), bf16),
            pltpu.VMEM((4, 1024, 512), bf16),
            pltpu.VMEM((N_CTX, 32, 512), bf16),
            pltpu.VMEM((N_CTX, 32, 512), bf16),
            pltpu.VMEM((N_CTX, 32, 512), f32),
            pltpu.VMEM((N_CTX, 32, 512), bf16),
            pltpu.VMEM((32, 8192), bf16),
            pltpu.SemaphoreType.DMA((2, 4)),
            pltpu.SemaphoreType.DMA((2, 4)),
            pltpu.SemaphoreType.DMA((2, 20)),
            pltpu.SemaphoreType.DMA((2, 32)),
            pltpu.SemaphoreType.DMA((4,)),
            pltpu.SemaphoreType.DMA((4,)),
            pltpu.SemaphoreType.DMA((N_CTX,)),
            pltpu.SemaphoreType.DMA((N_CTX,)),
            pltpu.SemaphoreType.DMA((3,)),
        ],
        compiler_params=pltpu.CompilerParams(
            collective_id=2, has_side_effects=True, vmem_limit_bytes=62 * MIB
        ),
        cost_estimate=pl.CostEstimate(
            flops=2 * 512 * 512 * 8192, bytes_accessed=20 * MIB, transcendentals=0
        ),
    )(attended, weight)

    all_table = tables[:, 0, :PAGE].reshape(-1)
    ctx_index = lax.axis_index("ctx")
    targets = ctx_index * 16 + jnp.arange(16, dtype=jnp.int32)
    matches = all_table[None, :] == targets[:, None]
    source = jnp.sum(
        jnp.where(matches, jnp.arange(all_table.shape[0], dtype=jnp.int32)[None, :], 0), axis=1
    )
    pages = new.reshape(2, 256, PAGE, D_HEAD)
    paged_kv = jnp.stack([pages[0][source], pages[1][source]], axis=2)
    return (projected, paged_kv)


def solution(mesh):
    return jax.shard_map(
        local,
        mesh=mesh,
        in_specs=(
            P("ctx", "tp"),
            P("ctx", "tp"),
            P("ctx", "tp"),
            P("ctx", "tp"),
            P("ctx", "tp"),
            P(),
            P("ctx"),
            P("tp", "ctx"),
        ),
        out_specs=(P(("ctx", "tp"), None), P("ctx", None, None, "tp")),
        check_vma=False,
    )
```

```python
import functools
import math

import jax
import jax.numpy as jnp
from jax import lax
from jax.experimental import pallas as pl
from jax.experimental.pallas import tpu as pltpu
from jax.sharding import PartitionSpec as P

HEADS = 64
KV_HEADS = 8
D_HEAD = 128
PAGE = 16
GROUP = HEADS // KV_HEADS
ROWS = 256
QROWS = ROWS * GROUP
CSH = 1024
N_CTX = 16
N_TP = 8
UNIT = 1024
BASE = N_CTX * CSH
TILE = 1024
EXPC = D_HEAD ** (-0.5) * math.log2(math.e)
MIB = 2**20


class Place:
    def __init__(self):
        c = lax.axis_index("ctx")
        self.c = c
        self.z = c // 4
        self.y = lax.rem(c // 2, 2)
        self.core = lax.rem(c, 2)
        self.zp = lax.rem(c + 4, 16)
        self.zm = lax.rem(c + 12, 16)
        self.z2 = lax.rem(c + 8, 16)
        self.dy = 2 - 4 * self.y
        self.dm = 1 - 2 * self.core
        self.yp = c + self.dy
        self.mate = c + self.dm
        self.cy, self.zmy, self.zpy, self.z2y = (
            slot + self.dy for slot in (c, self.zm, self.zp, self.z2)
        )


class Flow:
    def __init__(self, place, view, send, recv, kind, far="halves"):
        self.p, self.view, self.ss, self.rs = place, view, send, recv
        self.kind, self.far = kind, far
        self.sent = []

    def _copy(self, slot, part, dest, index):
        ref = self.view(slot, part)
        return pltpu.make_async_remote_copy(
            src_ref=ref,
            dst_ref=ref,
            send_sem=self.ss.at[index],
            recv_sem=self.rs.at[slot + (16 if part == 1 else 0)],
            device_id={"ctx": dest},
            device_id_type=pl.DeviceIdType.MESH,
        )

    def send(self, slot, part, dest):
        item = (slot, part, dest, len(self.sent))
        self.sent.append(item)
        self._copy(*item).start()

    def wait(self, slot, part=None):
        self._copy(slot, part, self.p.mate, 0).wait_recv()

    def finish(self):
        for item in self.sent:
            self._copy(*item).wait_send()

    def _along_z(self, slot):
        self.send(slot, None, self.p.zp)
        self.send(slot, None, self.p.zm)
        if self.far == "direct":
            self.send(slot, None, self.p.z2)

    def own(self):
        p = self.p
        if self.kind == "y":
            self.send(p.c, None, p.yp)
        self._along_z(p.c)
        if self.kind == "z":
            self.send(p.c, None, p.yp)
        self.send(p.c, None, p.mate)

    def _down(self, slot):
        if self.kind == "z":
            self.send(slot, None, self.p.yp)
        self.send(slot, None, self.p.mate)

    def y(self, slot):
        self.wait(slot)
        if self.kind == "y":
            self._along_z(slot)
        self.send(slot, None, self.p.mate)

    def from_zm(self, slot):
        self.wait(slot)
        if self.far == "halves":
            self.send(slot, 0, self.p.zp)
        self._down(slot)

    def from_zp(self, slot):
        self.wait(slot)
        if self.far == "halves":
            self.send(slot, 1, self.p.zm)
        self._down(slot)

    def from_z2(self, slot):
        if self.far == "halves":
            self.wait(slot, 0)
            self.wait(slot, 1)
        else:
            self.wait(slot)
        self._down(slot)


class Across:
    def __init__(self):
        t = lax.axis_index("tp")
        x = lax.rem(t, 4)
        self.t, self.x, self.h = t, x, t // 4
        self.rp, self.rm, self.r2 = (lax.rem(x + d, 4) for d in (1, 3, 2))
        self.xp, self.xm, self.x2 = (t - x + r for r in (self.rp, self.rm, self.r2))
        self.yh = lax.rem(t + 4, N_TP)


class Weight:
    def __init__(self, place, own, buf, send, recv):
        self.p, self.own, self.buf, self.ss, self.rs = place, own, buf, send, recv
        self.sent = []

    def _copy(self, src, slot, part, dest, index):
        rows = pl.ds(0, 1024) if part is None else pl.ds(part * 512, 512)
        dst = self.buf.at[slot, rows]
        return pltpu.make_async_remote_copy(
            src_ref=dst if src is None else src,
            dst_ref=dst,
            send_sem=self.ss.at[index],
            recv_sem=self.rs.at[slot + (4 if part == 1 else 0)],
            device_id={"tp": dest},
            device_id_type=pl.DeviceIdType.MESH,
        )

    def send(self, src, slot, part, dest):
        item = (src, slot, part, dest, len(self.sent))
        self.sent.append(item)
        self._copy(*item).start()

    def wait(self, slot, part=None):
        self._copy(None, slot, part, self.p.yh, 0).wait_recv()

    def start(self):
        self.send(self.own, self.p.x, None, self.p.xp)
        self.send(self.own, self.p.x, None, self.p.xm)

    def forward(self):
        self.wait(self.p.rm)
        self.send(None, self.p.rm, 0, self.p.xp)
        self.wait(self.p.rp)
        self.send(None, self.p.rp, 1, self.p.xm)

    def finish(self):
        self.wait(self.p.r2, 0)
        self.wait(self.p.r2, 1)
        for item in self.sent:
            self._copy(*item).wait_send()


def greet(partners):
    barrier = pltpu.get_barrier_semaphore()
    for partner in partners:
        pl.semaphore_signal(
            barrier, inc=1, device_id=partner, device_id_type=pl.DeviceIdType.MESH
        )
    pl.semaphore_wait(barrier, len(partners))


def attend(q, k, v, m_ref, l_ref, a_ref, rows, allowed=None):
    s = lax.dot_general(q, k, (((1,), (1,)), ((), ())), preferred_element_type=jnp.float32)
    if allowed is not None:
        s = jnp.where(allowed, s, -1e30)
    m = m_ref[rows, :]
    top = jnp.maximum(m, jnp.max(s, axis=1, keepdims=True))
    m_ref[rows, :] = top
    factor = jnp.exp2((m - top) * EXPC)
    w = jnp.exp2((s - jnp.tile(top, (1, s.shape[1] // 128))) * EXPC)
    part = functools.reduce(jnp.add, [w[:, i : i + 128] for i in range(0, w.shape[1], 128)])
    l_ref[rows, :] = l_ref[rows, :] * factor + part
    a_ref[rows, :] = a_ref[rows, :] * factor + jnp.dot(
        w.astype(jnp.bfloat16), v, preferred_element_type=jnp.float32
    )


def gather_attend(
    q_ref, sk_ref, sv_ref, ck_ref, cv_ref, t_ref, w_ref,
    m_ref, l_ref, a_ref, qs, ko_ref, vo_ref, so_ref, to_ref, wo_ref,
    kbuf, vbuf, tbuf, send, recv, tsend, trecv, wsend, wrecv, local,
):
    p = Place()
    across = Across()
    wt = Weight(across, w_ref, wo_ref, wsend, wrecv)

    def cached(buf):
        def view(slot, part):
            rows = CSH if part is None else CSH // 2
            first = slot * CSH + (CSH // 2 if part == 1 else 0)
            return buf.at[pl.ds(pl.multiple_of(first, CSH // 2), rows)]
        return view

    def stretch(buf):
        def view(slot, part):
            rows = ROWS if part is None else ROWS // 2
            first = BASE + slot * ROWS + (ROWS // 2 if part == 1 else 0)
            return buf.at[pl.ds(pl.multiple_of(first, ROWS // 2), rows)]
        return view

    sk = Flow(p, stretch(kbuf), send.at[0], recv.at[0], "y", "direct")
    sv = Flow(p, stretch(vbuf), send.at[1], recv.at[1], "y", "direct")
    ck = Flow(p, cached(kbuf), send.at[2], recv.at[2], "z")
    cv = Flow(p, cached(vbuf), send.at[3], recv.at[3], "y")
    tb = Flow(p, lambda slot, part: tbuf.at[slot], tsend, trecv, "z", "direct")

    own = [
        pltpu.make_async_copy(sk_ref, sk.view(p.c, None), local.at[0]),
        pltpu.make_async_copy(sv_ref, sv.view(p.c, None), local.at[1]),
        pltpu.make_async_copy(ck_ref, ck.view(p.c, None), local.at[2]),
        pltpu.make_async_copy(cv_ref, cv.view(p.c, None), local.at[3]),
    ]
    for copy in own:
        copy.start()
    wown = pltpu.make_async_copy(w_ref, wo_ref.at[across.x], local.at[4])
    wown.start()
    tbuf[p.c] = t_ref[...]
    greet(
        [{"ctx": x} for x in (p.zp, p.zm, p.z2, p.yp, p.mate)]
        + [{"tp": x} for x in (across.xp, across.xm)]
    )
    own[0].wait()
    own[1].wait()
    sv.own()
    sk.own()
    tb.own()
    wt.start()

    for h in range(GROUP):
        qs[pl.ds(h * ROWS, ROWS), :] = q_ref[:, pl.ds(h * D_HEAD, D_HEAD)]
    m_ref[...] = jnp.full_like(m_ref, -1e30)
    l_ref[...] = jnp.zeros_like(l_ref)
    a_ref[...] = jnp.zeros_like(a_ref)

    def mates(flow_k, flow_v, slot):
        flow_k.wait(slot)
        flow_v.wait(slot)

    def stretch_mates(group, y):
        mates(sk, sv, group * 4 + y * 2 + 1 - p.core)

    def first_stretch():
        sk.y(p.cy)
        sv.y(p.cy)
        own[2].wait()
        own[3].wait()
        ck.own()
        cv.own()
        for flow in (sk, sv):
            flow.from_zm(p.zm)
            flow.from_zp(p.zp)

    def far_stretch():
        for flow in (sk, sv):
            flow.from_z2(p.z2)

    def near_stretch_y():
        for flow in (sk, sv):
            flow.from_zm(p.zmy)
            flow.from_zp(p.zpy)

    def far_stretch_y():
        for flow in (sk, sv):
            flow.from_z2(p.z2y)

    def tables():
        tb.y(p.cy)
        for slot in (p.zm, p.zp, p.z2):
            tb.from_z2(slot)

    def tables_y():
        for slot in (p.zmy, p.zpy, p.z2y):
            tb.y(slot)

    def own_cached():
        cv.y(p.cy)
        ck.y(p.cy)

    def near_cached():
        for flow in (ck, cv):
            flow.from_zm(p.zm)
            flow.from_zp(p.zp)

    def far_cached():
        ck.from_z2(p.z2)
        cv.from_z2(p.z2)

    def near_cached_y():
        cv.from_zm(p.zmy)
        cv.from_zp(p.zpy)

    def more_cached_y():
        ck.y(p.zmy)
        ck.y(p.zpy)

    def far_cached_y():
        ck.y(p.z2y)
        cv.from_z2(p.z2y)

    outs = [
        pltpu.make_async_copy(kbuf.at[pl.ds(8 * CSH, 8 * CSH)], ko_ref, local.at[0]),
        pltpu.make_async_copy(vbuf.at[pl.ds(8 * CSH, 8 * CSH)], vo_ref, local.at[1]),
        pltpu.make_async_copy(kbuf.at[pl.ds(BASE, N_CTX * ROWS)], so_ref.at[0], local.at[2]),
        pltpu.make_async_copy(vbuf.at[pl.ds(BASE, N_CTX * ROWS)], so_ref.at[1], local.at[3]),
    ]

    def leftover():
        for slot in range(8, 16, 2):
            mates(ck, cv, slot + 1 - p.core)
        for group in range(4):
            @pl.when(group > p.z)
            def _():
                stretch_mates(group, 0)
                stretch_mates(group, 1)
        for copy in outs:
            copy.start()

    events = {
        1: first_stretch,
        2: far_stretch,
        3: near_stretch_y,
        4: far_stretch_y,
        6: own_cached,
        8: near_cached,
        10: wt.forward,
        12: far_cached,
        14: near_cached_y,
        15: more_cached_y,
        17: tables,
        19: far_cached_y,
        20: tables_y,
        23: leftover,
    }
    half = UNIT // 2
    first = lax.rem((p.z + 1) // 2, 2)

    def step(u, carry):
        for at, event in events.items():
            pl.when(u == at)(event)
        is_stretch = u < 2 * p.z + 2
        turn = jnp.where(u <= p.z, 0, 1)
        behind = jnp.maximum(p.z - u + turn * (p.z + 1), 0)
        pair = lax.rem(p.y + turn, 2)
        own_start = 2 * p.z + 2
        inside = p.z <= 1
        in_own = inside & (u >= own_start) & (u < own_start + 8)
        in_late = jnp.where(inside, (u >= 12) & (u < 20), u >= 8)
        late = jnp.maximum(u - 8, 0)
        other = jnp.maximum(u - 12, 0)
        mine = jnp.maximum(u - own_start, 0)
        group = jnp.where(in_own, first, jnp.where(inside | (lax.rem(late // 4, 2) == 1), 1 - first, first))
        column = jnp.where(in_own, mine // 4, jnp.where(inside, other // 4, late // 8))
        within = lax.rem(jnp.where(in_own, mine, late), 4)
        y = lax.rem(p.y + column, 2)
        core = lax.rem(p.core + within // 2, 2)
        slot = lax.rem(group * 4 + y * 2 + core, 16)

        @pl.when(is_stretch)
        def _():
            stretch_mates(behind, pair)

        @pl.when(jnp.logical_not(is_stretch) & (in_own | in_late) & (core != p.core) & (lax.rem(within, 2) == 0))
        def _():
            mates(ck, cv, slot)

        place = jnp.where(
            is_stretch,
            BASE + behind * UNIT + pair * half,
            slot * UNIT + lax.rem(within, 2) * half,
        )
        keys = pl.ds(pl.multiple_of(place, half), half)
        diagonal = is_stretch & (behind == p.z)

        @pl.when(diagonal)
        def _():
            token = lax.broadcasted_iota(jnp.int32, (QROWS, half), 0) % ROWS
            ahead = lax.broadcasted_iota(jnp.int32, (QROWS, half), 1)
            allowed = ahead + pair * half <= token + lax.rem(p.c, 4) * ROWS
            attend(qs[...], kbuf[keys, :], vbuf[keys, :], m_ref, l_ref, a_ref, slice(None), allowed)

        @pl.when(jnp.logical_not(diagonal) & (is_stretch | in_own | in_late))
        def _():
            attend(qs[...], kbuf[keys, :], vbuf[keys, :], m_ref, l_ref, a_ref, slice(None))

        return carry

    lax.fori_loop(0, 24, step, 0)

    for slot in range(0, 16, 2):
        tb.wait(slot + 1 - p.core)
    to_ref[...] = tbuf[...]
    for copy in outs:
        copy.wait()
    wown.wait()
    for flow in (sk, sv, ck, cv, tb, wt):
        flow.finish()


def finish_attend(
    len_ref, q_ref, k_ref, v_ref, m_in, l_in, a_in, o_ref, kbuf, vbuf, m_ref, l_ref, a_ref, qs, sem, ksem, vsem
):
    more = len_ref[0] - 8 * CSH
    whole = more // UNIT
    state = [
        pltpu.make_async_copy(src, dst, sem.at[i])
        for i, (src, dst) in enumerate(((q_ref, qs), (m_in, m_ref), (l_in, l_ref), (a_in, a_ref)))
    ]

    def fetch(u):
        keys = pl.ds(pl.multiple_of(u * UNIT, UNIT), UNIT)
        return (
            pltpu.make_async_copy(k_ref.at[keys], kbuf.at[keys], ksem.at[u]),
            pltpu.make_async_copy(v_ref.at[keys], vbuf.at[keys], vsem.at[u]),
        )

    for copy in (*state[:2], *fetch(0), *state[2:]):
        copy.start()
    for u in range(1, 8):
        for copy in fetch(u):
            copy.start()
    for copy in state:
        copy.wait()

    def step(u, allowed):
        for copy in fetch(u):
            copy.wait()
        keys = pl.ds(pl.multiple_of(u * UNIT, UNIT), UNIT)
        attend(qs[...], kbuf[keys, :], vbuf[keys, :], m_ref, l_ref, a_ref, slice(None), allowed)

    def whole_step(u, carry):
        step(u, None)
        return carry

    lax.fori_loop(0, whole, whole_step, 0)

    @pl.when(more - whole * UNIT > 0)
    def _():
        place = lax.broadcasted_iota(jnp.int32, (QROWS, UNIT), 1)
        step(whole, place < more - whole * UNIT)

    def unused(u, carry):
        for copy in fetch(u):
            copy.wait()
        return carry

    lax.fori_loop((more + UNIT - 1) // UNIT, 8, unused, 0)

    for h in range(GROUP):
        rows = pl.ds(h * ROWS, ROWS)
        total = jnp.sum(l_ref[rows, :], axis=1, keepdims=True)
        o_ref[:, pl.ds(h * D_HEAD, D_HEAD)] = (a_ref[rows, :] / total).astype(jnp.bfloat16)


def project(
    att_ref, w_ref, o_ref,
    x, w, pb, qb, keep, yb, ob,
    asend, arecv, send, recv, psend, precv, osend, orecv, local,
):
    p = Place()
    ac = Across()
    x_others = ((ac.rp, ac.xp), (ac.rm, ac.xm), (ac.r2, ac.x2))
    ctx_others = [lax.rem(p.c + d, N_CTX) for d in range(1, N_CTX)]
    wcopy = pltpu.make_async_copy(w_ref, w, local.at[0])
    wcopy.start()

    def rows_of(r, j):
        return pl.ds(pl.multiple_of((r + 4 * j) * 32, 32), 32)

    def cols_of(s, n):
        return pl.ds(pl.multiple_of(s * n, n), n)

    mine = [
        pltpu.make_async_copy(
            att_ref.at[rows_of(ac.x, j)], x.at[p.c, j, :, cols_of(ac.x, 1024)], local.at[1 + j]
        )
        for j in range(2)
    ]
    for copy in mine:
        copy.start()
    greet([{"tp": s} for s in (ac.xp, ac.xm, ac.x2, ac.yh)] + [{"ctx": s} for s in ctx_others])

    def swap(j, r, dest, source, index):
        return pltpu.make_async_remote_copy(
            src_ref=att_ref.at[rows_of(r, j)],
            dst_ref=x.at[p.c, j, :, cols_of(source, 1024)],
            send_sem=asend.at[j, index],
            recv_sem=arecv.at[j, source],
            device_id={"tp": dest},
            device_id_type=pl.DeviceIdType.MESH,
        )

    for j in (1, 0):
        for index, (r, dest) in enumerate(x_others):
            swap(j, r, dest, ac.x, index).start()

    def half(j):
        def view(slot, part):
            cols = pl.ds(0, 4096) if part is None else pl.ds(part * 2048, 2048)
            return x.at[slot, j, :, cols]
        return view

    fz = Flow(p, half(0), send.at[0], recv.at[0], "y")
    fy = Flow(p, half(1), send.at[1], recv.at[1], "y")
    for j, flow in ((1, fy), (0, fz)):
        mine[j].wait()
        for r, dest in x_others:
            swap(j, r, dest, r, 0).wait_recv()
        flow.own()

    def give(dest, source, index):
        return pltpu.make_async_remote_copy(
            src_ref=yb.at[dest],
            dst_ref=ob.at[:, cols_of(source, 512)],
            send_sem=osend.at[index],
            recv_sem=orecv.at[source],
            device_id={"ctx": dest},
            device_id_type=pl.DeviceIdType.MESH,
        )

    def cross(group):
        slots = pl.ds(group * 4, 4)
        return pltpu.make_async_remote_copy(
            src_ref=pb.at[slots],
            dst_ref=qb.at[slots],
            send_sem=psend.at[group],
            recv_sem=precv.at[group],
            device_id={"tp": ac.yh},
            device_id_type=pl.DeviceIdType.MESH,
        )

    def multiply(group):
        slots = pl.ds(group * 4, 4)
        for y in range(2):
            for flow in (fz, fy):
                flow.wait(group * 4 + y * 2 + 1 - p.core)

        def part(j):
            def step(k, total):
                a = x[slots, j, :, cols_of(k, 1024)].reshape(128, 1024)
                return total + jnp.dot(a, w[k], preferred_element_type=jnp.float32)

            return lax.fori_loop(0, 4, step, jnp.zeros((128, 512), jnp.float32)).reshape(4, 32, 512)

        pb[slots] = part(1 - ac.h).astype(jnp.bfloat16)
        cross(group).start()
        keep[slots] = part(ac.h)

    def combine(group):
        slots = pl.ds(group * 4, 4)
        cross(group).wait_recv()
        yb[slots] = (keep[slots] + qb[slots].astype(jnp.float32)).astype(jnp.bfloat16)
        for i in range(4):
            dest = group * 4 + i

            @pl.when(dest != p.c)
            def _():
                give(dest, p.c, dest).start()

    g0, gm, gp, g2 = p.z, p.zm // 4, p.zp // 4, p.z2 // 4
    both = (fy, fz)
    for flow in both:
        flow.y(p.cy)
    for flow in both:
        flow.from_zm(p.zm)
        flow.from_zp(p.zp)
    wcopy.wait()
    multiply(g0)
    for flow in both:
        flow.from_zm(p.zmy)
        flow.from_zp(p.zpy)
    combine(g0)
    ob[:, cols_of(p.c, 512)] = yb[p.c]
    multiply(gm)
    for flow in both:
        flow.from_z2(p.z2)
    multiply(gp)
    combine(gm)
    for flow in both:
        flow.from_z2(p.z2y)
    multiply(g2)
    combine(gp)
    combine(g2)

    for s in ctx_others:
        give(s, s, s).wait_recv()
    o_ref[...] = ob[...]
    for j in range(2):
        for index, (r, dest) in enumerate(x_others):
            swap(j, r, dest, ac.x, index).wait_send()
    for s in ctx_others:
        give(s, p.c, s).wait_send()
    for group in range(4):
        cross(group).wait_send()
    for flow in (fz, fy):
        flow.finish()


VMEM = pl.BlockSpec(memory_space=pltpu.VMEM)
ANY = pl.BlockSpec(memory_space=pl.ANY)


def local(
    queries,
    stretch_keys,
    stretch_values,
    cache_keys,
    cache_values,
    cached_len,
    page_table,
    out_weight,
):
    bf16, f32 = jnp.bfloat16, jnp.float32
    table = jnp.broadcast_to(jnp.pad(page_table, (0, 112))[None], (8, 128))
    state = jax.ShapeDtypeStruct((QROWS, D_HEAD), f32)
    m, l, a, heads, more_k, more_v, new, tables, weight = pl.pallas_call(
        gather_attend,
        name="gather_attend",
        out_shape=(
            state,
            state,
            state,
            jax.ShapeDtypeStruct((QROWS, D_HEAD), bf16),
            jax.ShapeDtypeStruct((8 * CSH, D_HEAD), bf16),
            jax.ShapeDtypeStruct((8 * CSH, D_HEAD), bf16),
            jax.ShapeDtypeStruct((2, N_CTX * ROWS, D_HEAD), bf16),
            jax.ShapeDtypeStruct((N_CTX, 8, 128), jnp.int32),
            jax.ShapeDtypeStruct((4, 1024, 512), bf16),
        ),
        in_specs=[VMEM, ANY, ANY, ANY, ANY, VMEM, ANY],
        out_specs=(VMEM, VMEM, VMEM, VMEM, ANY, ANY, ANY, VMEM, ANY),
        scratch_shapes=[
            pltpu.VMEM((BASE + N_CTX * ROWS, D_HEAD), bf16),
            pltpu.VMEM((BASE + N_CTX * ROWS, D_HEAD), bf16),
            pltpu.VMEM((N_CTX, 8, 128), jnp.int32),
            pltpu.SemaphoreType.DMA((4, 20)),
            pltpu.SemaphoreType.DMA((4, 32)),
            pltpu.SemaphoreType.DMA((20,)),
            pltpu.SemaphoreType.DMA((32,)),
            pltpu.SemaphoreType.DMA((8,)),
            pltpu.SemaphoreType.DMA((N_TP,)),
            pltpu.SemaphoreType.DMA((5,)),
        ],
        compiler_params=pltpu.CompilerParams(
            collective_id=1, has_side_effects=True, vmem_limit_bytes=62 * MIB
        ),
        cost_estimate=pl.CostEstimate(
            flops=4 * QROWS * 10 * UNIT * D_HEAD, bytes_accessed=20 * MIB, transcendentals=QROWS * 10 * UNIT
        ),
    )(queries, stretch_keys, stretch_values, cache_keys, cache_values, table, out_weight)

    attended = pl.pallas_call(
        finish_attend,
        name="finish_attend",
        out_shape=jax.ShapeDtypeStruct((ROWS, GROUP * D_HEAD), bf16),
        in_specs=[pl.BlockSpec(memory_space=pltpu.SMEM)] + [ANY] * 6,
        out_specs=VMEM,
        scratch_shapes=[
            pltpu.VMEM((8 * CSH, D_HEAD), bf16),
            pltpu.VMEM((8 * CSH, D_HEAD), bf16),
            pltpu.VMEM((QROWS, D_HEAD), f32),
            pltpu.VMEM((QROWS, D_HEAD), f32),
            pltpu.VMEM((QROWS, D_HEAD), f32),
            pltpu.VMEM((QROWS, D_HEAD), bf16),
            pltpu.SemaphoreType.DMA((4,)),
            pltpu.SemaphoreType.DMA((8,)),
            pltpu.SemaphoreType.DMA((8,)),
        ],
        compiler_params=pltpu.CompilerParams(vmem_limit_bytes=60 * MIB),
        cost_estimate=pl.CostEstimate(
            flops=4 * QROWS * 4 * UNIT * D_HEAD, bytes_accessed=8 * MIB, transcendentals=QROWS * 4 * UNIT
        ),
    )(cached_len, heads, more_k, more_v, m, l, a)

    projected = pl.pallas_call(
        project,
        name="project",
        out_shape=jax.ShapeDtypeStruct((32, 8192), bf16),
        in_specs=[ANY, ANY],
        out_specs=VMEM,
        scratch_shapes=[
            pltpu.VMEM((N_CTX, 2, 32, 4096), bf16),
            pltpu.VMEM((4, 1024, 512), bf16),
            pltpu.VMEM((N_CTX, 32, 512), bf16),
            pltpu.VMEM((N_CTX, 32, 512), bf16),
            pltpu.VMEM((N_CTX, 32, 512), f32),
            pltpu.VMEM((N_CTX, 32, 512), bf16),
            pltpu.VMEM((32, 8192), bf16),
            pltpu.SemaphoreType.DMA((2, 4)),
            pltpu.SemaphoreType.DMA((2, 4)),
            pltpu.SemaphoreType.DMA((2, 20)),
            pltpu.SemaphoreType.DMA((2, 32)),
            pltpu.SemaphoreType.DMA((4,)),
            pltpu.SemaphoreType.DMA((4,)),
            pltpu.SemaphoreType.DMA((N_CTX,)),
            pltpu.SemaphoreType.DMA((N_CTX,)),
            pltpu.SemaphoreType.DMA((3,)),
        ],
        compiler_params=pltpu.CompilerParams(
            collective_id=2, has_side_effects=True, vmem_limit_bytes=62 * MIB
        ),
        cost_estimate=pl.CostEstimate(
            flops=2 * 512 * 512 * 8192, bytes_accessed=20 * MIB, transcendentals=0
        ),
    )(attended, weight)

    all_table = tables[:, 0, :PAGE].reshape(-1)
    ctx_index = lax.axis_index("ctx")
    targets = ctx_index * 16 + jnp.arange(16, dtype=jnp.int32)
    matches = all_table[None, :] == targets[:, None]
    source = jnp.sum(
        jnp.where(matches, jnp.arange(all_table.shape[0], dtype=jnp.int32)[None, :], 0), axis=1
    )
    pages = new.reshape(2, 256, PAGE, D_HEAD)
    paged_kv = jnp.stack([pages[0][source], pages[1][source]], axis=2)
    return (projected, paged_kv)


def solution(mesh):
    return jax.shard_map(
        local,
        mesh=mesh,
        in_specs=(
            P("ctx", "tp"),
            P("ctx", "tp"),
            P("ctx", "tp"),
            P("ctx", "tp"),
            P("ctx", "tp"),
            P(),
            P("ctx"),
            P("tp", "ctx"),
        ),
        out_specs=(P(("ctx", "tp"), None), P("ctx", None, None, "tp")),
        check_vma=False,
    )
```

```python
import functools
import math

import jax
import jax.numpy as jnp
from jax import lax
from jax.experimental import pallas as pl
from jax.experimental.pallas import tpu as pltpu
from jax.sharding import PartitionSpec as P

HEADS = 64
KV_HEADS = 8
D_HEAD = 128
PAGE = 16
GROUP = HEADS // KV_HEADS
ROWS = 256
QROWS = ROWS * GROUP
CSH = 1024
N_CTX = 16
N_TP = 8
UNIT = 1024
BASE = N_CTX * CSH
TILE = 1024
EXPC = D_HEAD ** (-0.5) * math.log2(math.e)
MIB = 2**20


class Place:
    def __init__(self):
        c = lax.axis_index("ctx")
        self.c = c
        self.z = c // 4
        self.y = lax.rem(c // 2, 2)
        self.core = lax.rem(c, 2)
        self.zp = lax.rem(c + 4, 16)
        self.zm = lax.rem(c + 12, 16)
        self.z2 = lax.rem(c + 8, 16)
        self.dy = 2 - 4 * self.y
        self.dm = 1 - 2 * self.core
        self.yp = c + self.dy
        self.mate = c + self.dm
        self.cy, self.zmy, self.zpy, self.z2y = (
            slot + self.dy for slot in (c, self.zm, self.zp, self.z2)
        )


class Flow:
    def __init__(self, place, view, send, recv, kind, far="halves"):
        self.p, self.view, self.ss, self.rs = place, view, send, recv
        self.kind, self.far = kind, far
        self.sent = []

    def _copy(self, slot, part, dest, index):
        ref = self.view(slot, part)
        return pltpu.make_async_remote_copy(
            src_ref=ref,
            dst_ref=ref,
            send_sem=self.ss.at[index],
            recv_sem=self.rs.at[slot + (16 if part == 1 else 0)],
            device_id={"ctx": dest},
            device_id_type=pl.DeviceIdType.MESH,
        )

    def send(self, slot, part, dest):
        item = (slot, part, dest, len(self.sent))
        self.sent.append(item)
        self._copy(*item).start()

    def wait(self, slot, part=None):
        self._copy(slot, part, self.p.mate, 0).wait_recv()

    def finish(self):
        for item in self.sent:
            self._copy(*item).wait_send()

    def _along_z(self, slot):
        self.send(slot, None, self.p.zp)
        self.send(slot, None, self.p.zm)
        if self.far == "direct":
            self.send(slot, None, self.p.z2)

    def own(self):
        p = self.p
        if self.kind == "y":
            self.send(p.c, None, p.yp)
        self._along_z(p.c)
        if self.kind == "z":
            self.send(p.c, None, p.yp)
        self.send(p.c, None, p.mate)

    def _down(self, slot):
        if self.kind == "z":
            self.send(slot, None, self.p.yp)
        self.send(slot, None, self.p.mate)

    def y(self, slot):
        self.wait(slot)
        if self.kind == "y":
            self._along_z(slot)
        self.send(slot, None, self.p.mate)

    def from_zm(self, slot):
        self.wait(slot)
        if self.far == "halves":
            self.send(slot, 0, self.p.zp)
        self._down(slot)

    def from_zp(self, slot):
        self.wait(slot)
        if self.far == "halves":
            self.send(slot, 1, self.p.zm)
        self._down(slot)

    def from_z2(self, slot):
        if self.far == "halves":
            self.wait(slot, 0)
            self.wait(slot, 1)
        else:
            self.wait(slot)
        self._down(slot)


class Across:
    def __init__(self):
        t = lax.axis_index("tp")
        x = lax.rem(t, 4)
        self.t, self.x, self.h = t, x, t // 4
        self.rp, self.rm, self.r2 = (lax.rem(x + d, 4) for d in (1, 3, 2))
        self.xp, self.xm, self.x2 = (t - x + r for r in (self.rp, self.rm, self.r2))
        self.yh = lax.rem(t + 4, N_TP)


class Weight:
    def __init__(self, place, own, buf, send, recv):
        self.p, self.own, self.buf, self.ss, self.rs = place, own, buf, send, recv
        self.sent = []

    def _copy(self, src, slot, part, dest, index):
        rows = pl.ds(0, 1024) if part is None else pl.ds(part * 512, 512)
        dst = self.buf.at[slot, rows]
        return pltpu.make_async_remote_copy(
            src_ref=dst if src is None else src,
            dst_ref=dst,
            send_sem=self.ss.at[index],
            recv_sem=self.rs.at[slot + (4 if part == 1 else 0)],
            device_id={"tp": dest},
            device_id_type=pl.DeviceIdType.MESH,
        )

    def send(self, src, slot, part, dest):
        item = (src, slot, part, dest, len(self.sent))
        self.sent.append(item)
        self._copy(*item).start()

    def wait(self, slot, part=None):
        self._copy(None, slot, part, self.p.yh, 0).wait_recv()

    def start(self):
        self.send(self.own, self.p.x, None, self.p.xp)
        self.send(self.own, self.p.x, None, self.p.xm)

    def forward(self):
        self.wait(self.p.rm)
        self.send(None, self.p.rm, 0, self.p.xp)
        self.wait(self.p.rp)
        self.send(None, self.p.rp, 1, self.p.xm)

    def finish(self):
        self.wait(self.p.r2, 0)
        self.wait(self.p.r2, 1)
        for item in self.sent:
            self._copy(*item).wait_send()


def greet(partners):
    barrier = pltpu.get_barrier_semaphore()
    for partner in partners:
        pl.semaphore_signal(
            barrier, inc=1, device_id=partner, device_id_type=pl.DeviceIdType.MESH
        )
    pl.semaphore_wait(barrier, len(partners))


def attend(q, k, v, m_ref, l_ref, a_ref, rows, allowed=None):
    s = lax.dot_general(q, k, (((1,), (1,)), ((), ())), preferred_element_type=jnp.float32)
    if allowed is not None:
        s = jnp.where(allowed, s, -1e30)
    m = m_ref[rows, :]
    top = jnp.maximum(m, jnp.max(s, axis=1, keepdims=True))
    m_ref[rows, :] = top
    factor = jnp.exp2((m - top) * EXPC)
    w = jnp.exp2((s - jnp.tile(top, (1, s.shape[1] // 128))) * EXPC)
    part = functools.reduce(jnp.add, [w[:, i : i + 128] for i in range(0, w.shape[1], 128)])
    l_ref[rows, :] = l_ref[rows, :] * factor + part
    a_ref[rows, :] = a_ref[rows, :] * factor + jnp.dot(
        w.astype(jnp.bfloat16), v, preferred_element_type=jnp.float32
    )


def gather_attend(
    q_ref, sk_ref, sv_ref, ck_ref, cv_ref, t_ref, w_ref,
    m_ref, l_ref, a_ref, qs, ko_ref, vo_ref, so_ref, to_ref, wo_ref,
    kbuf, vbuf, tbuf, send, recv, tsend, trecv, wsend, wrecv, local,
):
    p = Place()
    across = Across()
    wt = Weight(across, w_ref, wo_ref, wsend, wrecv)

    def cached(buf):
        def view(slot, part):
            rows = CSH if part is None else CSH // 2
            first = slot * CSH + (CSH // 2 if part == 1 else 0)
            return buf.at[pl.ds(pl.multiple_of(first, CSH // 2), rows)]
        return view

    def stretch(buf):
        def view(slot, part):
            rows = ROWS if part is None else ROWS // 2
            first = BASE + slot * ROWS + (ROWS // 2 if part == 1 else 0)
            return buf.at[pl.ds(pl.multiple_of(first, ROWS // 2), rows)]
        return view

    sk = Flow(p, stretch(kbuf), send.at[0], recv.at[0], "y", "direct")
    sv = Flow(p, stretch(vbuf), send.at[1], recv.at[1], "y", "direct")
    ck = Flow(p, cached(kbuf), send.at[2], recv.at[2], "z")
    cv = Flow(p, cached(vbuf), send.at[3], recv.at[3], "y")
    tb = Flow(p, lambda slot, part: tbuf.at[slot], tsend, trecv, "z", "direct")

    own = [
        pltpu.make_async_copy(sk_ref, sk.view(p.c, None), local.at[0]),
        pltpu.make_async_copy(sv_ref, sv.view(p.c, None), local.at[1]),
        pltpu.make_async_copy(ck_ref, ck.view(p.c, None), local.at[2]),
        pltpu.make_async_copy(cv_ref, cv.view(p.c, None), local.at[3]),
    ]
    for copy in own:
        copy.start()
    wown = pltpu.make_async_copy(w_ref, wo_ref.at[across.x], local.at[4])
    wown.start()
    tbuf[p.c] = jnp.zeros((8, 128), jnp.int32)
    tbuf[p.c, 0:1, 0:PAGE] = t_ref[...]
    greet(
        [{"ctx": x} for x in (p.zp, p.zm, p.z2, p.yp, p.mate)]
        + [{"tp": x} for x in (across.xp, across.xm)]
    )
    own[0].wait()
    own[1].wait()
    sv.own()
    sk.own()
    tb.own()
    wt.start()

    for h in range(GROUP):
        qs[pl.ds(h * ROWS, ROWS), :] = q_ref[:, pl.ds(h * D_HEAD, D_HEAD)]
    m_ref[...] = jnp.full_like(m_ref, -1e30)
    l_ref[...] = jnp.zeros_like(l_ref)
    a_ref[...] = jnp.zeros_like(a_ref)

    def mates(flow_k, flow_v, slot):
        flow_k.wait(slot)
        flow_v.wait(slot)

    def stretch_mates(group, y):
        mates(sk, sv, group * 4 + y * 2 + 1 - p.core)

    def first_stretch():
        sk.y(p.cy)
        sv.y(p.cy)
        own[2].wait()
        own[3].wait()
        ck.own()
        cv.own()
        for flow in (sk, sv):
            flow.from_zm(p.zm)
            flow.from_zp(p.zp)

    def far_stretch():
        for flow in (sk, sv):
            flow.from_z2(p.z2)

    def near_stretch_y():
        for flow in (sk, sv):
            flow.from_zm(p.zmy)
            flow.from_zp(p.zpy)

    def far_stretch_y():
        for flow in (sk, sv):
            flow.from_z2(p.z2y)

    def tables():
        tb.y(p.cy)
        for slot in (p.zm, p.zp, p.z2):
            tb.from_z2(slot)

    def tables_y():
        for slot in (p.zmy, p.zpy, p.z2y):
            tb.y(slot)

    def own_cached():
        cv.y(p.cy)
        ck.y(p.cy)

    def near_cached():
        for flow in (ck, cv):
            flow.from_zm(p.zm)
            flow.from_zp(p.zp)

    def far_cached():
        ck.from_z2(p.z2)
        cv.from_z2(p.z2)

    def near_cached_y():
        cv.from_zm(p.zmy)
        cv.from_zp(p.zpy)

    def more_cached_y():
        ck.y(p.zmy)
        ck.y(p.zpy)

    def far_cached_y():
        ck.y(p.z2y)
        cv.from_z2(p.z2y)

    outs = [
        pltpu.make_async_copy(kbuf.at[pl.ds(8 * CSH, 8 * CSH)], ko_ref, local.at[0]),
        pltpu.make_async_copy(vbuf.at[pl.ds(8 * CSH, 8 * CSH)], vo_ref, local.at[1]),
        pltpu.make_async_copy(kbuf.at[pl.ds(BASE, N_CTX * ROWS)], so_ref.at[0], local.at[2]),
        pltpu.make_async_copy(vbuf.at[pl.ds(BASE, N_CTX * ROWS)], so_ref.at[1], local.at[3]),
    ]

    def sources():
        for slot in range(0, 16, 2):
            tb.wait(slot + 1 - p.core)
        table = tbuf[:, 0, :]
        lane = lax.broadcasted_iota(jnp.int32, (N_CTX, 128), 1)
        page = lax.broadcasted_iota(jnp.int32, (N_CTX, 128), 0) * PAGE + lane
        for slot in range(PAGE):
            found = (table == p.c * PAGE + slot) & (lane < PAGE)
            to_ref[slot] = jnp.sum(jnp.where(found, page, 0))

    def leftover():
        for slot in range(8, 16, 2):
            mates(ck, cv, slot + 1 - p.core)
        for group in range(4):
            @pl.when(group > p.z)
            def _():
                stretch_mates(group, 0)
                stretch_mates(group, 1)
        for copy in outs:
            copy.start()

    events = {
        1: first_stretch,
        2: far_stretch,
        3: near_stretch_y,
        4: far_stretch_y,
        6: own_cached,
        8: near_cached,
        10: wt.forward,
        12: far_cached,
        14: near_cached_y,
        15: more_cached_y,
        17: tables,
        19: far_cached_y,
        20: tables_y,
        22: sources,
        23: leftover,
    }
    half = UNIT // 2
    first = lax.rem((p.z + 1) // 2, 2)

    def step(u, carry):
        for at, event in events.items():
            pl.when(u == at)(event)
        is_stretch = u < 2 * p.z + 2
        turn = jnp.where(u <= p.z, 0, 1)
        behind = jnp.maximum(p.z - u + turn * (p.z + 1), 0)
        pair = lax.rem(p.y + turn, 2)
        own_start = 2 * p.z + 2
        inside = p.z <= 1
        in_own = inside & (u >= own_start) & (u < own_start + 8)
        in_late = jnp.where(inside, (u >= 12) & (u < 20), u >= 8)
        late = jnp.maximum(u - 8, 0)
        other = jnp.maximum(u - 12, 0)
        mine = jnp.maximum(u - own_start, 0)
        group = jnp.where(in_own, first, jnp.where(inside | (lax.rem(late // 4, 2) == 1), 1 - first, first))
        column = jnp.where(in_own, mine // 4, jnp.where(inside, other // 4, late // 8))
        within = lax.rem(jnp.where(in_own, mine, late), 4)
        y = lax.rem(p.y + column, 2)
        core = lax.rem(p.core + within // 2, 2)
        slot = lax.rem(group * 4 + y * 2 + core, 16)

        @pl.when(is_stretch)
        def _():
            stretch_mates(behind, pair)

        @pl.when(jnp.logical_not(is_stretch) & (in_own | in_late) & (core != p.core) & (lax.rem(within, 2) == 0))
        def _():
            mates(ck, cv, slot)

        place = jnp.where(
            is_stretch,
            BASE + behind * UNIT + pair * half,
            slot * UNIT + lax.rem(within, 2) * half,
        )
        keys = pl.ds(pl.multiple_of(place, half), half)
        diagonal = is_stretch & (behind == p.z)

        @pl.when(diagonal)
        def _():
            token = lax.broadcasted_iota(jnp.int32, (QROWS, half), 0) % ROWS
            ahead = lax.broadcasted_iota(jnp.int32, (QROWS, half), 1)
            allowed = ahead + pair * half <= token + lax.rem(p.c, 4) * ROWS
            attend(qs[...], kbuf[keys, :], vbuf[keys, :], m_ref, l_ref, a_ref, slice(None), allowed)

        @pl.when(jnp.logical_not(diagonal) & (is_stretch | in_own | in_late))
        def _():
            attend(qs[...], kbuf[keys, :], vbuf[keys, :], m_ref, l_ref, a_ref, slice(None))

        return carry

    lax.fori_loop(0, 24, step, 0)

    for copy in outs:
        copy.wait()
    wown.wait()
    for flow in (sk, sv, ck, cv, tb, wt):
        flow.finish()


def finish_attend(
    len_ref, t_ref, q_ref, k_ref, v_ref, m_in, l_in, a_in, new_ref,
    o_ref, p_ref,
    kbuf, vbuf, m_ref, l_ref, a_ref, qs, sem, ksem, vsem, psem,
):
    more = len_ref[0] - 8 * CSH
    whole = more // UNIT
    state = [
        pltpu.make_async_copy(src, dst, sem.at[i])
        for i, (src, dst) in enumerate(((q_ref, qs), (m_in, m_ref), (l_in, l_ref), (a_in, a_ref)))
    ]

    def fetch(u):
        keys = pl.ds(pl.multiple_of(u * UNIT, UNIT), UNIT)
        return (
            pltpu.make_async_copy(k_ref.at[keys], kbuf.at[keys], ksem.at[u]),
            pltpu.make_async_copy(v_ref.at[keys], vbuf.at[keys], vsem.at[u]),
        )

    for copy in (*state[:2], *fetch(0), *state[2:]):
        copy.start()
    for u in range(1, 8):
        for copy in fetch(u):
            copy.start()

    def page(kind, source, slot):
        return pltpu.make_async_copy(
            new_ref.at[kind, pl.ds(pl.multiple_of(source * PAGE, PAGE), PAGE)],
            p_ref.at[slot, :, pl.ds(kind * D_HEAD, D_HEAD)],
            psem.at[kind, slot],
        )

    for slot in range(PAGE):
        for kind in range(2):
            page(kind, t_ref[slot], slot).start()
    for copy in state:
        copy.wait()

    def step(u, allowed):
        for copy in fetch(u):
            copy.wait()
        keys = pl.ds(pl.multiple_of(u * UNIT, UNIT), UNIT)
        attend(qs[...], kbuf[keys, :], vbuf[keys, :], m_ref, l_ref, a_ref, slice(None), allowed)

    def whole_step(u, carry):
        step(u, None)
        return carry

    lax.fori_loop(0, whole, whole_step, 0)

    @pl.when(more - whole * UNIT > 0)
    def _():
        place = lax.broadcasted_iota(jnp.int32, (QROWS, UNIT), 1)
        step(whole, place < more - whole * UNIT)

    def unused(u, carry):
        for copy in fetch(u):
            copy.wait()
        return carry

    lax.fori_loop((more + UNIT - 1) // UNIT, 8, unused, 0)

    for h in range(GROUP):
        rows = pl.ds(h * ROWS, ROWS)
        total = jnp.sum(l_ref[rows, :], axis=1, keepdims=True)
        o_ref[:, pl.ds(h * D_HEAD, D_HEAD)] = (a_ref[rows, :] / total).astype(jnp.bfloat16)
    for kind in range(2):
        for slot in range(PAGE):
            page(kind, 0, slot).wait()


def project(
    att_ref, w_ref, o_ref,
    x, w, pb, qb, keep, yb, ob,
    asend, arecv, send, recv, psend, precv, osend, orecv, local,
):
    p = Place()
    ac = Across()
    x_others = ((ac.rp, ac.xp), (ac.rm, ac.xm), (ac.r2, ac.x2))
    ctx_others = [lax.rem(p.c + d, N_CTX) for d in range(1, N_CTX)]
    wcopy = pltpu.make_async_copy(w_ref, w, local.at[0])
    wcopy.start()

    def rows_of(r, j):
        return pl.ds(pl.multiple_of((r + 4 * j) * 32, 32), 32)

    def cols_of(s, n):
        return pl.ds(pl.multiple_of(s * n, n), n)

    mine = [
        pltpu.make_async_copy(
            att_ref.at[rows_of(ac.x, j)], x.at[p.c, j, :, cols_of(ac.x, 1024)], local.at[1 + j]
        )
        for j in range(2)
    ]
    for copy in mine:
        copy.start()
    greet([{"tp": s} for s in (ac.xp, ac.xm, ac.x2, ac.yh)] + [{"ctx": s} for s in ctx_others])

    def swap(j, r, dest, source, index):
        return pltpu.make_async_remote_copy(
            src_ref=att_ref.at[rows_of(r, j)],
            dst_ref=x.at[p.c, j, :, cols_of(source, 1024)],
            send_sem=asend.at[j, index],
            recv_sem=arecv.at[j, source],
            device_id={"tp": dest},
            device_id_type=pl.DeviceIdType.MESH,
        )

    for j in (1, 0):
        for index, (r, dest) in enumerate(x_others):
            swap(j, r, dest, ac.x, index).start()

    def half(j):
        def view(slot, part):
            cols = pl.ds(0, 4096) if part is None else pl.ds(part * 2048, 2048)
            return x.at[slot, j, :, cols]
        return view

    fz = Flow(p, half(0), send.at[0], recv.at[0], "y")
    fy = Flow(p, half(1), send.at[1], recv.at[1], "y")
    for j, flow in ((1, fy), (0, fz)):
        mine[j].wait()
        for r, dest in x_others:
            swap(j, r, dest, r, 0).wait_recv()
        flow.own()

    def give(dest, source, index):
        return pltpu.make_async_remote_copy(
            src_ref=yb.at[dest],
            dst_ref=ob.at[:, cols_of(source, 512)],
            send_sem=osend.at[index],
            recv_sem=orecv.at[source],
            device_id={"ctx": dest},
            device_id_type=pl.DeviceIdType.MESH,
        )

    def cross(group):
        slots = pl.ds(group * 4, 4)
        return pltpu.make_async_remote_copy(
            src_ref=pb.at[slots],
            dst_ref=qb.at[slots],
            send_sem=psend.at[group],
            recv_sem=precv.at[group],
            device_id={"tp": ac.yh},
            device_id_type=pl.DeviceIdType.MESH,
        )

    def multiply(group):
        slots = pl.ds(group * 4, 4)
        for y in range(2):
            for flow in (fz, fy):
                flow.wait(group * 4 + y * 2 + 1 - p.core)

        def part(j):
            def step(k, total):
                a = x[slots, j, :, cols_of(k, 1024)].reshape(128, 1024)
                return total + jnp.dot(a, w[k], preferred_element_type=jnp.float32)

            return lax.fori_loop(0, 4, step, jnp.zeros((128, 512), jnp.float32)).reshape(4, 32, 512)

        pb[slots] = part(1 - ac.h).astype(jnp.bfloat16)
        cross(group).start()
        keep[slots] = part(ac.h)

    def combine(group):
        slots = pl.ds(group * 4, 4)
        cross(group).wait_recv()
        yb[slots] = (keep[slots] + qb[slots].astype(jnp.float32)).astype(jnp.bfloat16)
        for i in range(4):
            dest = group * 4 + i

            @pl.when(dest != p.c)
            def _():
                give(dest, p.c, dest).start()

    g0, gm, gp, g2 = p.z, p.zm // 4, p.zp // 4, p.z2 // 4
    both = (fy, fz)
    for flow in both:
        flow.y(p.cy)
    for flow in both:
        flow.from_zm(p.zm)
        flow.from_zp(p.zp)
    wcopy.wait()
    multiply(g0)
    for flow in both:
        flow.from_zm(p.zmy)
        flow.from_zp(p.zpy)
    combine(g0)
    ob[:, cols_of(p.c, 512)] = yb[p.c]
    multiply(gm)
    for flow in both:
        flow.from_z2(p.z2)
    multiply(gp)
    combine(gm)
    for flow in both:
        flow.from_z2(p.z2y)
    multiply(g2)
    combine(gp)
    combine(g2)

    for s in ctx_others:
        give(s, s, s).wait_recv()
    o_ref[...] = ob[...]
    for j in range(2):
        for index, (r, dest) in enumerate(x_others):
            swap(j, r, dest, ac.x, index).wait_send()
    for s in ctx_others:
        give(s, p.c, s).wait_send()
    for group in range(4):
        cross(group).wait_send()
    for flow in (fz, fy):
        flow.finish()


VMEM = pl.BlockSpec(memory_space=pltpu.VMEM)
ANY = pl.BlockSpec(memory_space=pl.ANY)
SMEM = pl.BlockSpec(memory_space=pltpu.SMEM)


def local(
    queries,
    stretch_keys,
    stretch_values,
    cache_keys,
    cache_values,
    cached_len,
    page_table,
    out_weight,
):
    bf16, f32 = jnp.bfloat16, jnp.float32
    state = jax.ShapeDtypeStruct((QROWS, D_HEAD), f32)
    m, l, a, heads, more_k, more_v, new, sources, weight = pl.pallas_call(
        gather_attend,
        name="gather_attend",
        out_shape=(
            state,
            state,
            state,
            jax.ShapeDtypeStruct((QROWS, D_HEAD), bf16),
            jax.ShapeDtypeStruct((8 * CSH, D_HEAD), bf16),
            jax.ShapeDtypeStruct((8 * CSH, D_HEAD), bf16),
            jax.ShapeDtypeStruct((2, N_CTX * ROWS, D_HEAD), bf16),
            jax.ShapeDtypeStruct((PAGE,), jnp.int32),
            jax.ShapeDtypeStruct((4, 1024, 512), bf16),
        ),
        in_specs=[VMEM, ANY, ANY, ANY, ANY, VMEM, ANY],
        out_specs=(VMEM, VMEM, VMEM, VMEM, ANY, ANY, ANY, SMEM, ANY),
        scratch_shapes=[
            pltpu.VMEM((BASE + N_CTX * ROWS, D_HEAD), bf16),
            pltpu.VMEM((BASE + N_CTX * ROWS, D_HEAD), bf16),
            pltpu.VMEM((N_CTX, 8, 128), jnp.int32),
            pltpu.SemaphoreType.DMA((4, 20)),
            pltpu.SemaphoreType.DMA((4, 32)),
            pltpu.SemaphoreType.DMA((20,)),
            pltpu.SemaphoreType.DMA((32,)),
            pltpu.SemaphoreType.DMA((8,)),
            pltpu.SemaphoreType.DMA((N_TP,)),
            pltpu.SemaphoreType.DMA((5,)),
        ],
        compiler_params=pltpu.CompilerParams(
            collective_id=1, has_side_effects=True, vmem_limit_bytes=62 * MIB
        ),
        cost_estimate=pl.CostEstimate(
            flops=4 * QROWS * 10 * UNIT * D_HEAD, bytes_accessed=20 * MIB, transcendentals=QROWS * 10 * UNIT
        ),
    )(queries, stretch_keys, stretch_values, cache_keys, cache_values, page_table.reshape(1, PAGE), out_weight)

    attended, pages = pl.pallas_call(
        finish_attend,
        name="finish_attend",
        out_shape=(
            jax.ShapeDtypeStruct((ROWS, GROUP * D_HEAD), bf16),
            jax.ShapeDtypeStruct((PAGE, PAGE, 2 * D_HEAD), bf16),
        ),
        in_specs=[SMEM] * 2 + [ANY] * 7,
        out_specs=(VMEM, ANY),
        scratch_shapes=[
            pltpu.VMEM((8 * CSH, D_HEAD), bf16),
            pltpu.VMEM((8 * CSH, D_HEAD), bf16),
            pltpu.VMEM((QROWS, D_HEAD), f32),
            pltpu.VMEM((QROWS, D_HEAD), f32),
            pltpu.VMEM((QROWS, D_HEAD), f32),
            pltpu.VMEM((QROWS, D_HEAD), bf16),
            pltpu.SemaphoreType.DMA((4,)),
            pltpu.SemaphoreType.DMA((8,)),
            pltpu.SemaphoreType.DMA((8,)),
            pltpu.SemaphoreType.DMA((2, PAGE)),
        ],
        compiler_params=pltpu.CompilerParams(vmem_limit_bytes=60 * MIB),
        cost_estimate=pl.CostEstimate(
            flops=4 * QROWS * 4 * UNIT * D_HEAD, bytes_accessed=8 * MIB, transcendentals=QROWS * 4 * UNIT
        ),
    )(cached_len, sources, heads, more_k, more_v, m, l, a, new)

    projected = pl.pallas_call(
        project,
        name="project",
        out_shape=jax.ShapeDtypeStruct((32, 8192), bf16),
        in_specs=[ANY, ANY],
        out_specs=VMEM,
        scratch_shapes=[
            pltpu.VMEM((N_CTX, 2, 32, 4096), bf16),
            pltpu.VMEM((4, 1024, 512), bf16),
            pltpu.VMEM((N_CTX, 32, 512), bf16),
            pltpu.VMEM((N_CTX, 32, 512), bf16),
            pltpu.VMEM((N_CTX, 32, 512), f32),
            pltpu.VMEM((N_CTX, 32, 512), bf16),
            pltpu.VMEM((32, 8192), bf16),
            pltpu.SemaphoreType.DMA((2, 4)),
            pltpu.SemaphoreType.DMA((2, 4)),
            pltpu.SemaphoreType.DMA((2, 20)),
            pltpu.SemaphoreType.DMA((2, 32)),
            pltpu.SemaphoreType.DMA((4,)),
            pltpu.SemaphoreType.DMA((4,)),
            pltpu.SemaphoreType.DMA((N_CTX,)),
            pltpu.SemaphoreType.DMA((N_CTX,)),
            pltpu.SemaphoreType.DMA((3,)),
        ],
        compiler_params=pltpu.CompilerParams(
            collective_id=2, has_side_effects=True, vmem_limit_bytes=62 * MIB
        ),
        cost_estimate=pl.CostEstimate(
            flops=2 * 512 * 512 * 8192, bytes_accessed=20 * MIB, transcendentals=0
        ),
    )(attended, weight)

    paged_kv = pages.reshape(PAGE, PAGE, 2, D_HEAD)
    return (projected, paged_kv)


def solution(mesh):
    return jax.shard_map(
        local,
        mesh=mesh,
        in_specs=(
            P("ctx", "tp"),
            P("ctx", "tp"),
            P("ctx", "tp"),
            P("ctx", "tp"),
            P("ctx", "tp"),
            P(),
            P("ctx"),
            P("tp", "ctx"),
        ),
        out_specs=(P(("ctx", "tp"), None), P("ctx", None, None, "tp")),
        check_vma=False,
    )
```

```python
import functools
import math

import jax
import jax.numpy as jnp
from jax import lax
from jax.experimental import pallas as pl
from jax.experimental.pallas import tpu as pltpu
from jax.sharding import PartitionSpec as P

HEADS = 64
KV_HEADS = 8
D_HEAD = 128
PAGE = 16
GROUP = HEADS // KV_HEADS
ROWS = 256
QROWS = ROWS * GROUP
CSH = 1024
N_CTX = 16
N_TP = 8
UNIT = 1024
BASE = N_CTX * CSH
SROWS = ROWS + 16
TILE = 1024
EXPC = D_HEAD ** (-0.5) * math.log2(math.e)
MIB = 2**20


class Place:
    def __init__(self):
        c = lax.axis_index("ctx")
        self.c = c
        self.z = c // 4
        self.y = lax.rem(c // 2, 2)
        self.core = lax.rem(c, 2)
        self.zp = lax.rem(c + 4, 16)
        self.zm = lax.rem(c + 12, 16)
        self.z2 = lax.rem(c + 8, 16)
        self.dy = 2 - 4 * self.y
        self.dm = 1 - 2 * self.core
        self.yp = c + self.dy
        self.mate = c + self.dm
        self.cy, self.zmy, self.zpy, self.z2y = (
            slot + self.dy for slot in (c, self.zm, self.zp, self.z2)
        )


class Flow:
    def __init__(self, place, view, send, recv, kind, far="halves"):
        self.p, self.view, self.ss, self.rs = place, view, send, recv
        self.kind, self.far = kind, far
        self.sent = []

    def _copy(self, slot, part, dest, index):
        ref = self.view(slot, part)
        return pltpu.make_async_remote_copy(
            src_ref=ref,
            dst_ref=ref,
            send_sem=self.ss.at[index],
            recv_sem=self.rs.at[slot + (16 if part == 1 else 0)],
            device_id={"ctx": dest},
            device_id_type=pl.DeviceIdType.MESH,
        )

    def send(self, slot, part, dest):
        item = (slot, part, dest, len(self.sent))
        self.sent.append(item)
        self._copy(*item).start()

    def wait(self, slot, part=None):
        self._copy(slot, part, self.p.mate, 0).wait_recv()

    def finish(self):
        for item in self.sent:
            self._copy(*item).wait_send()

    def _along_z(self, slot):
        self.send(slot, None, self.p.zp)
        self.send(slot, None, self.p.zm)
        if self.far == "direct":
            self.send(slot, None, self.p.z2)

    def own(self):
        p = self.p
        if self.kind == "y":
            self.send(p.c, None, p.yp)
        self._along_z(p.c)
        if self.kind == "z":
            self.send(p.c, None, p.yp)
        self.send(p.c, None, p.mate)

    def _down(self, slot):
        if self.kind == "z":
            self.send(slot, None, self.p.yp)
        self.send(slot, None, self.p.mate)

    def y(self, slot):
        self.wait(slot)
        if self.kind == "y":
            self._along_z(slot)
        self.send(slot, None, self.p.mate)

    def from_zm(self, slot):
        self.wait(slot)
        if self.far == "halves":
            self.send(slot, 0, self.p.zp)
        self._down(slot)

    def from_zp(self, slot):
        self.wait(slot)
        if self.far == "halves":
            self.send(slot, 1, self.p.zm)
        self._down(slot)

    def from_z2(self, slot):
        if self.far == "halves":
            self.wait(slot, 0)
            self.wait(slot, 1)
        else:
            self.wait(slot)
        self._down(slot)


class Across:
    def __init__(self):
        t = lax.axis_index("tp")
        x = lax.rem(t, 4)
        self.t, self.x, self.h = t, x, t // 4
        self.rp, self.rm, self.r2 = (lax.rem(x + d, 4) for d in (1, 3, 2))
        self.xp, self.xm, self.x2 = (t - x + r for r in (self.rp, self.rm, self.r2))
        self.yh = lax.rem(t + 4, N_TP)


class Weight:
    def __init__(self, place, own, buf, send, recv):
        self.p, self.own, self.buf, self.ss, self.rs = place, own, buf, send, recv
        self.sent = []

    def _copy(self, src, slot, part, dest, index):
        rows = pl.ds(0, 1024) if part is None else pl.ds(part * 512, 512)
        dst = self.buf.at[slot, rows]
        return pltpu.make_async_remote_copy(
            src_ref=dst if src is None else src,
            dst_ref=dst,
            send_sem=self.ss.at[index],
            recv_sem=self.rs.at[slot + (4 if part == 1 else 0)],
            device_id={"tp": dest},
            device_id_type=pl.DeviceIdType.MESH,
        )

    def send(self, src, slot, part, dest):
        item = (src, slot, part, dest, len(self.sent))
        self.sent.append(item)
        self._copy(*item).start()

    def wait(self, slot, part=None):
        self._copy(None, slot, part, self.p.yh, 0).wait_recv()

    def start(self):
        self.send(self.own, self.p.x, None, self.p.xp)
        self.send(self.own, self.p.x, None, self.p.xm)

    def forward(self):
        self.wait(self.p.rm)
        self.send(None, self.p.rm, 0, self.p.xp)
        self.wait(self.p.rp)
        self.send(None, self.p.rp, 1, self.p.xm)

    def finish(self):
        self.wait(self.p.r2, 0)
        self.wait(self.p.r2, 1)
        for item in self.sent:
            self._copy(*item).wait_send()


def greet(partners):
    barrier = pltpu.get_barrier_semaphore()
    for partner in partners:
        pl.semaphore_signal(
            barrier, inc=1, device_id=partner, device_id_type=pl.DeviceIdType.MESH
        )
    pl.semaphore_wait(barrier, len(partners))


def attend(q, k, v, m_ref, l_ref, a_ref, rows, allowed=None):
    s = lax.dot_general(q, k, (((1,), (1,)), ((), ())), preferred_element_type=jnp.float32)
    if allowed is not None:
        s = jnp.where(allowed, s, -1e30)
    m = m_ref[rows, :]
    top = jnp.maximum(m, jnp.max(s, axis=1, keepdims=True))
    m_ref[rows, :] = top
    factor = jnp.exp2((m - top) * EXPC)
    w = jnp.exp2((s - jnp.tile(top, (1, s.shape[1] // 128))) * EXPC)
    part = functools.reduce(jnp.add, [w[:, i : i + 128] for i in range(0, w.shape[1], 128)])
    l_ref[rows, :] = l_ref[rows, :] * factor + part
    a_ref[rows, :] = a_ref[rows, :] * factor + jnp.dot(
        w.astype(jnp.bfloat16), v, preferred_element_type=jnp.float32
    )


def gather_attend(
    q_ref, sk_ref, sv_ref, ck_ref, cv_ref, t_ref, w_ref,
    m_ref, l_ref, a_ref, qs, ko_ref, vo_ref, so_ref, to_ref, wo_ref,
    kbuf, vbuf, sbuf, send, recv, wsend, wrecv, local,
):
    p = Place()
    across = Across()
    wt = Weight(across, w_ref, wo_ref, wsend, wrecv)

    def cached(buf):
        def view(slot, part):
            rows = CSH if part is None else CSH // 2
            first = slot * CSH + (CSH // 2 if part == 1 else 0)
            return buf.at[pl.ds(pl.multiple_of(first, CSH // 2), rows)]
        return view

    st = Flow(p, lambda slot, part: sbuf.at[slot], send.at[0], recv.at[0], "y", "direct")
    ck = Flow(p, cached(kbuf), send.at[1], recv.at[1], "z")
    cv = Flow(p, cached(vbuf), send.at[2], recv.at[2], "y")

    own = [
        pltpu.make_async_copy(sk_ref, sbuf.at[p.c, pl.ds(0, ROWS), pl.ds(0, D_HEAD)], local.at[0]),
        pltpu.make_async_copy(
            sv_ref, sbuf.at[p.c, pl.ds(0, ROWS), pl.ds(D_HEAD, D_HEAD)], local.at[1]
        ),
        pltpu.make_async_copy(ck_ref, ck.view(p.c, None), local.at[2]),
        pltpu.make_async_copy(cv_ref, cv.view(p.c, None), local.at[3]),
    ]
    for copy in own:
        copy.start()
    wown = pltpu.make_async_copy(w_ref, wo_ref.at[across.x], local.at[4])
    wown.start()
    sbuf[p.c, ROWS:SROWS, :] = jnp.zeros((16, 2 * D_HEAD), jnp.bfloat16)
    entries = jnp.broadcast_to(t_ref[...].astype(jnp.float32), (16, PAGE))
    sbuf[p.c, ROWS:SROWS, 0:PAGE] = entries.astype(jnp.bfloat16)
    greet(
        [{"ctx": x} for x in (p.zp, p.zm, p.z2, p.yp, p.mate)]
        + [{"tp": x} for x in (across.xp, across.xm)]
    )
    own[0].wait()
    own[1].wait()
    st.own()
    wt.start()

    for h in range(GROUP):
        qs[pl.ds(h * ROWS, ROWS), :] = q_ref[:, pl.ds(h * D_HEAD, D_HEAD)]
    m_ref[...] = jnp.full_like(m_ref, -1e30)
    l_ref[...] = jnp.zeros_like(l_ref)
    a_ref[...] = jnp.zeros_like(a_ref)

    def mates(flow_k, flow_v, slot):
        flow_k.wait(slot)
        flow_v.wait(slot)

    def stretch_mates(group, y):
        st.wait(group * 4 + y * 2 + 1 - p.core)

    def first_stretch():
        st.y(p.cy)
        own[2].wait()
        own[3].wait()
        ck.own()
        cv.own()
        st.from_zm(p.zm)
        st.from_zp(p.zp)

    def far_stretch():
        st.from_z2(p.z2)

    def near_stretch_y():
        st.from_zm(p.zmy)
        st.from_zp(p.zpy)

    def far_stretch_y():
        st.from_z2(p.z2y)

    def own_cached():
        cv.y(p.cy)
        ck.y(p.cy)

    def near_cached():
        for flow in (ck, cv):
            flow.from_zm(p.zm)
            flow.from_zp(p.zp)

    def far_cached():
        ck.from_z2(p.z2)
        cv.from_z2(p.z2)

    def near_cached_y():
        cv.from_zm(p.zmy)
        cv.from_zp(p.zpy)

    def more_cached_y():
        ck.y(p.zmy)
        ck.y(p.zpy)

    def far_cached_y():
        ck.y(p.z2y)
        cv.from_z2(p.z2y)

    outs = [
        pltpu.make_async_copy(kbuf.at[pl.ds(8 * CSH, 8 * CSH)], ko_ref, local.at[0]),
        pltpu.make_async_copy(vbuf.at[pl.ds(8 * CSH, 8 * CSH)], vo_ref, local.at[1]),
        pltpu.make_async_copy(sbuf, so_ref, local.at[2]),
    ]

    def sources():
        table = sbuf[:, ROWS:SROWS, 0:128][:, 0, :].astype(jnp.float32)
        lane = lax.broadcasted_iota(jnp.int32, (N_CTX, 128), 1)
        page = lax.broadcasted_iota(jnp.int32, (N_CTX, 128), 0) * PAGE + lane
        for slot in range(PAGE):
            found = (table == (p.c * PAGE + slot).astype(jnp.float32)) & (lane < PAGE)
            to_ref[slot] = jnp.sum(jnp.where(found, page, 0))

    def leftover():
        for slot in range(8, 16, 2):
            mates(ck, cv, slot + 1 - p.core)
        for group in range(4):
            @pl.when(group > p.z)
            def _():
                stretch_mates(group, 0)
                stretch_mates(group, 1)
        for copy in outs:
            copy.start()
        sources()

    events = {
        1: first_stretch,
        2: far_stretch,
        3: near_stretch_y,
        4: far_stretch_y,
        6: own_cached,
        8: near_cached,
        10: wt.forward,
        12: far_cached,
        14: near_cached_y,
        15: more_cached_y,
        19: far_cached_y,
        23: leftover,
    }
    half = UNIT // 2
    first = lax.rem((p.z + 1) // 2, 2)

    def step(u, carry):
        for at, event in events.items():
            pl.when(u == at)(event)
        is_stretch = u < 2 * p.z + 2
        turn = jnp.where(u <= p.z, 0, 1)
        behind = jnp.maximum(p.z - u + turn * (p.z + 1), 0)
        pair = lax.rem(p.y + turn, 2)
        own_start = 2 * p.z + 2
        inside = p.z <= 1
        in_own = inside & (u >= own_start) & (u < own_start + 8)
        in_late = jnp.where(inside, (u >= 12) & (u < 20), u >= 8)
        late = jnp.maximum(u - 8, 0)
        other = jnp.maximum(u - 12, 0)
        mine = jnp.maximum(u - own_start, 0)
        group = jnp.where(in_own, first, jnp.where(inside | (lax.rem(late // 4, 2) == 1), 1 - first, first))
        column = jnp.where(in_own, mine // 4, jnp.where(inside, other // 4, late // 8))
        within = lax.rem(jnp.where(in_own, mine, late), 4)
        y = lax.rem(p.y + column, 2)
        core = lax.rem(p.core + within // 2, 2)
        slot = lax.rem(group * 4 + y * 2 + core, 16)

        @pl.when(is_stretch)
        def _():
            stretch_mates(behind, pair)

        @pl.when(jnp.logical_not(is_stretch) & (in_own | in_late) & (core != p.core) & (lax.rem(within, 2) == 0))
        def _():
            mates(ck, cv, slot)

        def new_pair():
            pieces = [sbuf[behind * 4 + pair * 2 + i, 0:ROWS, :] for i in range(2)]
            both = jnp.concatenate(pieces, axis=0)
            return both[:, :D_HEAD], both[:, D_HEAD:]

        @pl.when(is_stretch & (behind == p.z))
        def _():
            k, v = new_pair()
            token = lax.broadcasted_iota(jnp.int32, (QROWS, half), 0) % ROWS
            ahead = lax.broadcasted_iota(jnp.int32, (QROWS, half), 1)
            allowed = ahead + pair * half <= token + lax.rem(p.c, 4) * ROWS
            attend(qs[...], k, v, m_ref, l_ref, a_ref, slice(None), allowed)

        @pl.when(is_stretch & (behind != p.z))
        def _():
            k, v = new_pair()
            attend(qs[...], k, v, m_ref, l_ref, a_ref, slice(None))

        @pl.when(jnp.logical_not(is_stretch) & (in_own | in_late))
        def _():
            keys = pl.ds(pl.multiple_of(slot * UNIT + lax.rem(within, 2) * half, half), half)
            attend(qs[...], kbuf[keys, :], vbuf[keys, :], m_ref, l_ref, a_ref, slice(None))

        return carry

    lax.fori_loop(0, 24, step, 0)

    for copy in outs:
        copy.wait()
    wown.wait()
    for flow in (st, ck, cv, wt):
        flow.finish()


def finish_attend(
    len_ref, t_ref, q_ref, k_ref, v_ref, m_in, l_in, a_in, new_ref,
    o_ref, p_ref,
    kbuf, vbuf, m_ref, l_ref, a_ref, qs, sem, ksem, vsem, psem,
):
    more = len_ref[0] - 8 * CSH
    whole = more // UNIT
    state = [
        pltpu.make_async_copy(src, dst, sem.at[i])
        for i, (src, dst) in enumerate(((q_ref, qs), (m_in, m_ref), (l_in, l_ref), (a_in, a_ref)))
    ]

    def fetch(u):
        keys = pl.ds(pl.multiple_of(u * UNIT, UNIT), UNIT)
        return (
            pltpu.make_async_copy(k_ref.at[keys], kbuf.at[keys], ksem.at[u]),
            pltpu.make_async_copy(v_ref.at[keys], vbuf.at[keys], vsem.at[u]),
        )

    for copy in (*state[:2], *fetch(0), *state[2:]):
        copy.start()
    for u in range(1, 8):
        for copy in fetch(u):
            copy.start()

    def page(source, slot):
        rows = pl.ds(pl.multiple_of(lax.rem(source, PAGE) * PAGE, PAGE), PAGE)
        return pltpu.make_async_copy(new_ref.at[source // PAGE, rows], p_ref.at[slot], psem.at[slot])

    for slot in range(PAGE):
        page(t_ref[slot], slot).start()
    for copy in state:
        copy.wait()

    def step(u, allowed):
        for copy in fetch(u):
            copy.wait()
        keys = pl.ds(pl.multiple_of(u * UNIT, UNIT), UNIT)
        attend(qs[...], kbuf[keys, :], vbuf[keys, :], m_ref, l_ref, a_ref, slice(None), allowed)

    def whole_step(u, carry):
        step(u, None)
        return carry

    lax.fori_loop(0, whole, whole_step, 0)

    @pl.when(more - whole * UNIT > 0)
    def _():
        place = lax.broadcasted_iota(jnp.int32, (QROWS, UNIT), 1)
        step(whole, place < more - whole * UNIT)

    def unused(u, carry):
        for copy in fetch(u):
            copy.wait()
        return carry

    lax.fori_loop((more + UNIT - 1) // UNIT, 8, unused, 0)

    for h in range(GROUP):
        rows = pl.ds(h * ROWS, ROWS)
        total = jnp.sum(l_ref[rows, :], axis=1, keepdims=True)
        o_ref[:, pl.ds(h * D_HEAD, D_HEAD)] = (a_ref[rows, :] / total).astype(jnp.bfloat16)
    for slot in range(PAGE):
        page(0, slot).wait()


def project(
    att_ref, w_ref, o_ref,
    x, w, pb, qb, keep, yb, ob,
    asend, arecv, send, recv, psend, precv, osend, orecv, local,
):
    p = Place()
    ac = Across()
    x_others = ((ac.rp, ac.xp), (ac.rm, ac.xm), (ac.r2, ac.x2))
    ctx_others = [lax.rem(p.c + d, N_CTX) for d in range(1, N_CTX)]
    wcopy = pltpu.make_async_copy(w_ref, w, local.at[0])
    wcopy.start()

    def rows_of(r, j):
        return pl.ds(pl.multiple_of((r + 4 * j) * 32, 32), 32)

    def cols_of(s, n):
        return pl.ds(pl.multiple_of(s * n, n), n)

    mine = [
        pltpu.make_async_copy(
            att_ref.at[rows_of(ac.x, j)], x.at[p.c, j, :, cols_of(ac.x, 1024)], local.at[1 + j]
        )
        for j in range(2)
    ]
    for copy in mine:
        copy.start()
    greet([{"tp": s} for s in (ac.xp, ac.xm, ac.x2, ac.yh)] + [{"ctx": s} for s in ctx_others])

    def swap(j, r, dest, source, index):
        return pltpu.make_async_remote_copy(
            src_ref=att_ref.at[rows_of(r, j)],
            dst_ref=x.at[p.c, j, :, cols_of(source, 1024)],
            send_sem=asend.at[j, index],
            recv_sem=arecv.at[j, source],
            device_id={"tp": dest},
            device_id_type=pl.DeviceIdType.MESH,
        )

    for j in (1, 0):
        for index, (r, dest) in enumerate(x_others):
            swap(j, r, dest, ac.x, index).start()

    def half(j):
        def view(slot, part):
            cols = pl.ds(0, 4096) if part is None else pl.ds(part * 2048, 2048)
            return x.at[slot, j, :, cols]
        return view

    fz = Flow(p, half(0), send.at[0], recv.at[0], "y")
    fy = Flow(p, half(1), send.at[1], recv.at[1], "y")
    for j, flow in ((1, fy), (0, fz)):
        mine[j].wait()
        for r, dest in x_others:
            swap(j, r, dest, r, 0).wait_recv()
        flow.own()

    def give(dest, source, index):
        return pltpu.make_async_remote_copy(
            src_ref=yb.at[dest],
            dst_ref=ob.at[:, cols_of(source, 512)],
            send_sem=osend.at[index],
            recv_sem=orecv.at[source],
            device_id={"ctx": dest},
            device_id_type=pl.DeviceIdType.MESH,
        )

    def cross(group):
        slots = pl.ds(group * 4, 4)
        return pltpu.make_async_remote_copy(
            src_ref=pb.at[slots],
            dst_ref=qb.at[slots],
            send_sem=psend.at[group],
            recv_sem=precv.at[group],
            device_id={"tp": ac.yh},
            device_id_type=pl.DeviceIdType.MESH,
        )

    def multiply(group):
        slots = pl.ds(group * 4, 4)
        for y in range(2):
            for flow in (fz, fy):
                flow.wait(group * 4 + y * 2 + 1 - p.core)

        def part(j):
            def step(k, total):
                a = x[slots, j, :, cols_of(k, 1024)].reshape(128, 1024)
                return total + jnp.dot(a, w[k], preferred_element_type=jnp.float32)

            return lax.fori_loop(0, 4, step, jnp.zeros((128, 512), jnp.float32)).reshape(4, 32, 512)

        pb[slots] = part(1 - ac.h).astype(jnp.bfloat16)
        cross(group).start()
        keep[slots] = part(ac.h)

    def combine(group):
        slots = pl.ds(group * 4, 4)
        cross(group).wait_recv()
        yb[slots] = (keep[slots] + qb[slots].astype(jnp.float32)).astype(jnp.bfloat16)
        for i in range(4):
            dest = group * 4 + i

            @pl.when(dest != p.c)
            def _():
                give(dest, p.c, dest).start()

    g0, gm, gp, g2 = p.z, p.zm // 4, p.zp // 4, p.z2 // 4
    both = (fy, fz)
    for flow in both:
        flow.y(p.cy)
    for flow in both:
        flow.from_zm(p.zm)
        flow.from_zp(p.zp)
    wcopy.wait()
    multiply(g0)
    for flow in both:
        flow.from_zm(p.zmy)
        flow.from_zp(p.zpy)
    combine(g0)
    ob[:, cols_of(p.c, 512)] = yb[p.c]
    multiply(gm)
    for flow in both:
        flow.from_z2(p.z2)
    multiply(gp)
    combine(gm)
    for flow in both:
        flow.from_z2(p.z2y)
    multiply(g2)
    combine(gp)
    combine(g2)

    for s in ctx_others:
        give(s, s, s).wait_recv()
    o_ref[...] = ob[...]
    for j in range(2):
        for index, (r, dest) in enumerate(x_others):
            swap(j, r, dest, ac.x, index).wait_send()
    for s in ctx_others:
        give(s, p.c, s).wait_send()
    for group in range(4):
        cross(group).wait_send()
    for flow in (fz, fy):
        flow.finish()


VMEM = pl.BlockSpec(memory_space=pltpu.VMEM)
ANY = pl.BlockSpec(memory_space=pl.ANY)
SMEM = pl.BlockSpec(memory_space=pltpu.SMEM)


def local(
    queries,
    stretch_keys,
    stretch_values,
    cache_keys,
    cache_values,
    cached_len,
    page_table,
    out_weight,
):
    bf16, f32 = jnp.bfloat16, jnp.float32
    state = jax.ShapeDtypeStruct((QROWS, D_HEAD), f32)
    m, l, a, heads, more_k, more_v, new, sources, weight = pl.pallas_call(
        gather_attend,
        name="gather_attend",
        out_shape=(
            state,
            state,
            state,
            jax.ShapeDtypeStruct((QROWS, D_HEAD), bf16),
            jax.ShapeDtypeStruct((8 * CSH, D_HEAD), bf16),
            jax.ShapeDtypeStruct((8 * CSH, D_HEAD), bf16),
            jax.ShapeDtypeStruct((N_CTX, SROWS, 2 * D_HEAD), bf16),
            jax.ShapeDtypeStruct((PAGE,), jnp.int32),
            jax.ShapeDtypeStruct((4, 1024, 512), bf16),
        ),
        in_specs=[VMEM, ANY, ANY, ANY, ANY, VMEM, ANY],
        out_specs=(VMEM, VMEM, VMEM, VMEM, ANY, ANY, ANY, SMEM, ANY),
        scratch_shapes=[
            pltpu.VMEM((BASE, D_HEAD), bf16),
            pltpu.VMEM((BASE, D_HEAD), bf16),
            pltpu.VMEM((N_CTX, SROWS, 2 * D_HEAD), bf16),
            pltpu.SemaphoreType.DMA((3, 20)),
            pltpu.SemaphoreType.DMA((3, 32)),
            pltpu.SemaphoreType.DMA((8,)),
            pltpu.SemaphoreType.DMA((N_TP,)),
            pltpu.SemaphoreType.DMA((5,)),
        ],
        compiler_params=pltpu.CompilerParams(
            collective_id=1, has_side_effects=True, vmem_limit_bytes=62 * MIB
        ),
        cost_estimate=pl.CostEstimate(
            flops=4 * QROWS * 10 * UNIT * D_HEAD, bytes_accessed=20 * MIB, transcendentals=QROWS * 10 * UNIT
        ),
    )(queries, stretch_keys, stretch_values, cache_keys, cache_values, page_table.reshape(1, PAGE), out_weight)

    attended, pages = pl.pallas_call(
        finish_attend,
        name="finish_attend",
        out_shape=(
            jax.ShapeDtypeStruct((ROWS, GROUP * D_HEAD), bf16),
            jax.ShapeDtypeStruct((PAGE, PAGE, 2 * D_HEAD), bf16),
        ),
        in_specs=[SMEM] * 2 + [ANY] * 7,
        out_specs=(VMEM, ANY),
        scratch_shapes=[
            pltpu.VMEM((8 * CSH, D_HEAD), bf16),
            pltpu.VMEM((8 * CSH, D_HEAD), bf16),
            pltpu.VMEM((QROWS, D_HEAD), f32),
            pltpu.VMEM((QROWS, D_HEAD), f32),
            pltpu.VMEM((QROWS, D_HEAD), f32),
            pltpu.VMEM((QROWS, D_HEAD), bf16),
            pltpu.SemaphoreType.DMA((4,)),
            pltpu.SemaphoreType.DMA((8,)),
            pltpu.SemaphoreType.DMA((8,)),
            pltpu.SemaphoreType.DMA((PAGE,)),
        ],
        compiler_params=pltpu.CompilerParams(vmem_limit_bytes=60 * MIB),
        cost_estimate=pl.CostEstimate(
            flops=4 * QROWS * 4 * UNIT * D_HEAD, bytes_accessed=8 * MIB, transcendentals=QROWS * 4 * UNIT
        ),
    )(cached_len, sources, heads, more_k, more_v, m, l, a, new)

    projected = pl.pallas_call(
        project,
        name="project",
        out_shape=jax.ShapeDtypeStruct((32, 8192), bf16),
        in_specs=[ANY, ANY],
        out_specs=VMEM,
        scratch_shapes=[
            pltpu.VMEM((N_CTX, 2, 32, 4096), bf16),
            pltpu.VMEM((4, 1024, 512), bf16),
            pltpu.VMEM((N_CTX, 32, 512), bf16),
            pltpu.VMEM((N_CTX, 32, 512), bf16),
            pltpu.VMEM((N_CTX, 32, 512), f32),
            pltpu.VMEM((N_CTX, 32, 512), bf16),
            pltpu.VMEM((32, 8192), bf16),
            pltpu.SemaphoreType.DMA((2, 4)),
            pltpu.SemaphoreType.DMA((2, 4)),
            pltpu.SemaphoreType.DMA((2, 20)),
            pltpu.SemaphoreType.DMA((2, 32)),
            pltpu.SemaphoreType.DMA((4,)),
            pltpu.SemaphoreType.DMA((4,)),
            pltpu.SemaphoreType.DMA((N_CTX,)),
            pltpu.SemaphoreType.DMA((N_CTX,)),
            pltpu.SemaphoreType.DMA((3,)),
        ],
        compiler_params=pltpu.CompilerParams(
            collective_id=2, has_side_effects=True, vmem_limit_bytes=62 * MIB
        ),
        cost_estimate=pl.CostEstimate(
            flops=2 * 512 * 512 * 8192, bytes_accessed=20 * MIB, transcendentals=0
        ),
    )(attended, weight)

    paged_kv = pages.reshape(PAGE, PAGE, 2, D_HEAD)
    return (projected, paged_kv)


def solution(mesh):
    return jax.shard_map(
        local,
        mesh=mesh,
        in_specs=(
            P("ctx", "tp"),
            P("ctx", "tp"),
            P("ctx", "tp"),
            P("ctx", "tp"),
            P("ctx", "tp"),
            P(),
            P("ctx"),
            P("tp", "ctx"),
        ),
        out_specs=(P(("ctx", "tp"), None), P("ctx", None, None, "tp")),
        check_vma=False,
    )
```

```python
import functools
import math

import jax
import jax.numpy as jnp
from jax import lax
from jax.experimental import pallas as pl
from jax.experimental.pallas import tpu as pltpu
from jax.sharding import PartitionSpec as P

HEADS = 64
KV_HEADS = 8
D_HEAD = 128
PAGE = 16
GROUP = HEADS // KV_HEADS
ROWS = 256
QROWS = ROWS * GROUP
CSH = 1024
N_CTX = 16
N_TP = 8
UNIT = 1024
BASE = N_CTX * CSH
SROWS = ROWS + 16
TILE = 1024
EXPC = D_HEAD ** (-0.5) * math.log2(math.e)
MIB = 2**20


class Place:
    def __init__(self):
        c = lax.axis_index("ctx")
        self.c = c
        self.z = c // 4
        self.y = lax.rem(c // 2, 2)
        self.core = lax.rem(c, 2)
        self.zp = lax.rem(c + 4, 16)
        self.zm = lax.rem(c + 12, 16)
        self.z2 = lax.rem(c + 8, 16)
        self.dy = 2 - 4 * self.y
        self.dm = 1 - 2 * self.core
        self.yp = c + self.dy
        self.mate = c + self.dm
        self.cy, self.zmy, self.zpy, self.z2y = (
            slot + self.dy for slot in (c, self.zm, self.zp, self.z2)
        )


class Flow:
    def __init__(self, place, view, send, recv, kind, far="halves"):
        self.p, self.view, self.ss, self.rs = place, view, send, recv
        self.kind, self.far = kind, far
        self.sent = []

    def _copy(self, slot, part, dest, index):
        ref = self.view(slot, part)
        return pltpu.make_async_remote_copy(
            src_ref=ref,
            dst_ref=ref,
            send_sem=self.ss.at[index],
            recv_sem=self.rs.at[slot + (16 if part == 1 else 0)],
            device_id={"ctx": dest},
            device_id_type=pl.DeviceIdType.MESH,
        )

    def send(self, slot, part, dest):
        item = (slot, part, dest, len(self.sent))
        self.sent.append(item)
        self._copy(*item).start()

    def wait(self, slot, part=None):
        self._copy(slot, part, self.p.mate, 0).wait_recv()

    def finish(self):
        for item in self.sent:
            self._copy(*item).wait_send()

    def _along_z(self, slot):
        self.send(slot, None, self.p.zp)
        self.send(slot, None, self.p.zm)
        if self.far == "direct":
            self.send(slot, None, self.p.z2)

    def own(self):
        p = self.p
        if self.kind == "y":
            self.send(p.c, None, p.yp)
        self._along_z(p.c)
        if self.kind == "z":
            self.send(p.c, None, p.yp)
        self.send(p.c, None, p.mate)

    def _down(self, slot):
        if self.kind == "z":
            self.send(slot, None, self.p.yp)
        self.send(slot, None, self.p.mate)

    def y(self, slot):
        self.wait(slot)
        if self.kind == "y":
            self._along_z(slot)
        self.send(slot, None, self.p.mate)

    def from_zm(self, slot):
        self.wait(slot)
        if self.far == "halves":
            self.send(slot, 0, self.p.zp)
        self._down(slot)

    def from_zp(self, slot):
        self.wait(slot)
        if self.far == "halves":
            self.send(slot, 1, self.p.zm)
        self._down(slot)

    def from_z2(self, slot):
        if self.far == "halves":
            self.wait(slot, 0)
            self.wait(slot, 1)
        else:
            self.wait(slot)
        self._down(slot)


class Across:
    def __init__(self):
        t = lax.axis_index("tp")
        x = lax.rem(t, 4)
        self.t, self.x, self.h = t, x, t // 4
        self.rp, self.rm, self.r2 = (lax.rem(x + d, 4) for d in (1, 3, 2))
        self.xp, self.xm, self.x2 = (t - x + r for r in (self.rp, self.rm, self.r2))
        self.yh = lax.rem(t + 4, N_TP)


class Weight:
    def __init__(self, place, own, buf, send, recv):
        self.p, self.own, self.buf, self.ss, self.rs = place, own, buf, send, recv
        self.sent = []

    def _copy(self, src, slot, part, dest, index):
        rows = pl.ds(0, 1024) if part is None else pl.ds(part * 512, 512)
        dst = self.buf.at[slot, rows]
        return pltpu.make_async_remote_copy(
            src_ref=dst if src is None else src,
            dst_ref=dst,
            send_sem=self.ss.at[index],
            recv_sem=self.rs.at[slot + (4 if part == 1 else 0)],
            device_id={"tp": dest},
            device_id_type=pl.DeviceIdType.MESH,
        )

    def send(self, src, slot, part, dest):
        item = (src, slot, part, dest, len(self.sent))
        self.sent.append(item)
        self._copy(*item).start()

    def wait(self, slot, part=None):
        self._copy(None, slot, part, self.p.yh, 0).wait_recv()

    def start(self):
        self.send(self.own, self.p.x, None, self.p.xp)
        self.send(self.own, self.p.x, None, self.p.xm)

    def forward(self):
        self.wait(self.p.rm)
        self.send(None, self.p.rm, 0, self.p.xp)
        self.wait(self.p.rp)
        self.send(None, self.p.rp, 1, self.p.xm)

    def finish(self):
        self.wait(self.p.r2, 0)
        self.wait(self.p.r2, 1)
        for item in self.sent:
            self._copy(*item).wait_send()


def greet(partners):
    barrier = pltpu.get_barrier_semaphore()
    for partner in partners:
        pl.semaphore_signal(
            barrier, inc=1, device_id=partner, device_id_type=pl.DeviceIdType.MESH
        )
    pl.semaphore_wait(barrier, len(partners))


def attend(q, k, v, m_ref, l_ref, a_ref, rows, allowed=None):
    s = lax.dot_general(q, k, (((1,), (1,)), ((), ())), preferred_element_type=jnp.float32)
    if allowed is not None:
        s = jnp.where(allowed, s, -1e30)
    m = m_ref[rows, :]
    top = jnp.maximum(m, jnp.max(s, axis=1, keepdims=True))
    m_ref[rows, :] = top
    factor = jnp.exp2((m - top) * EXPC)
    w = jnp.exp2((s - jnp.tile(top, (1, s.shape[1] // 128))) * EXPC)
    part = functools.reduce(jnp.add, [w[:, i : i + 128] for i in range(0, w.shape[1], 128)])
    l_ref[rows, :] = l_ref[rows, :] * factor + part
    a_ref[rows, :] = a_ref[rows, :] * factor + jnp.dot(
        w.astype(jnp.bfloat16), v, preferred_element_type=jnp.float32
    )


def gather_attend(
    q_ref, sk_ref, sv_ref, ck_ref, cv_ref, t_ref, w_ref,
    m_ref, l_ref, a_ref, qs, ko_ref, vo_ref, so_ref, to_ref, wo_ref,
    kbuf, vbuf, sbuf, send, recv, wsend, wrecv, local,
):
    p = Place()
    across = Across()
    wt = Weight(across, w_ref, wo_ref, wsend, wrecv)

    def cached(buf):
        def view(slot, part):
            rows = CSH if part is None else CSH // 2
            first = slot * CSH + (CSH // 2 if part == 1 else 0)
            return buf.at[pl.ds(pl.multiple_of(first, CSH // 2), rows)]
        return view

    st = Flow(p, lambda slot, part: sbuf.at[slot], send.at[0], recv.at[0], "y", "direct")
    ck = Flow(p, cached(kbuf), send.at[1], recv.at[1], "z")
    cv = Flow(p, cached(vbuf), send.at[2], recv.at[2], "y")

    own = [
        pltpu.make_async_copy(sk_ref, sbuf.at[p.c, pl.ds(0, ROWS), pl.ds(0, D_HEAD)], local.at[0]),
        pltpu.make_async_copy(
            sv_ref, sbuf.at[p.c, pl.ds(0, ROWS), pl.ds(D_HEAD, D_HEAD)], local.at[1]
        ),
        pltpu.make_async_copy(ck_ref, ck.view(p.c, None), local.at[2]),
        pltpu.make_async_copy(cv_ref, cv.view(p.c, None), local.at[3]),
    ]
    for copy in own:
        copy.start()
    wown = pltpu.make_async_copy(w_ref, wo_ref.at[across.x], local.at[4])
    wown.start()
    sbuf[p.c, ROWS:SROWS, :] = jnp.zeros((16, 2 * D_HEAD), jnp.bfloat16)
    entries = jnp.broadcast_to(t_ref[...].astype(jnp.float32), (16, PAGE))
    sbuf[p.c, ROWS:SROWS, 0:PAGE] = entries.astype(jnp.bfloat16)
    greet(
        [{"ctx": x} for x in (p.zp, p.zm, p.z2, p.yp, p.mate)]
        + [{"tp": x} for x in (across.xp, across.xm)]
    )
    own[0].wait()
    own[1].wait()
    st.own()
    wt.start()

    for h in range(GROUP):
        qs[pl.ds(h * ROWS, ROWS), :] = q_ref[:, pl.ds(h * D_HEAD, D_HEAD)]
    m_ref[...] = jnp.full_like(m_ref, -1e30)
    l_ref[...] = jnp.zeros_like(l_ref)
    a_ref[...] = jnp.zeros_like(a_ref)

    def mates(flow_k, flow_v, slot):
        flow_k.wait(slot)
        flow_v.wait(slot)

    def stretch_mates(group, y):
        st.wait(group * 4 + y * 2 + 1 - p.core)

    def first_stretch():
        st.y(p.cy)
        own[2].wait()
        own[3].wait()
        ck.own()
        cv.own()
        st.from_zm(p.zm)
        st.from_zp(p.zp)

    def far_stretch():
        st.from_z2(p.z2)

    def near_stretch_y():
        st.from_zm(p.zmy)
        st.from_zp(p.zpy)

    def far_stretch_y():
        st.from_z2(p.z2y)

    def own_cached():
        cv.y(p.cy)
        ck.y(p.cy)

    def near_cached():
        for flow in (ck, cv):
            flow.from_zm(p.zm)
            flow.from_zp(p.zp)

    def far_cached():
        ck.from_z2(p.z2)
        cv.from_z2(p.z2)

    def near_cached_y():
        cv.from_zm(p.zmy)
        cv.from_zp(p.zpy)

    def more_cached_y():
        ck.y(p.zmy)
        ck.y(p.zpy)

    def far_cached_y():
        ck.y(p.z2y)
        cv.from_z2(p.z2y)

    outs = [
        pltpu.make_async_copy(kbuf.at[pl.ds(8 * CSH, 8 * CSH)], ko_ref, local.at[0]),
        pltpu.make_async_copy(vbuf.at[pl.ds(8 * CSH, 8 * CSH)], vo_ref, local.at[1]),
        pltpu.make_async_copy(sbuf, so_ref, local.at[2]),
    ]

    def sources():
        table = sbuf[:, ROWS:SROWS, 0:128][:, 0, :].astype(jnp.float32)
        lane = lax.broadcasted_iota(jnp.int32, (N_CTX, 128), 1)
        page = lax.broadcasted_iota(jnp.int32, (N_CTX, 128), 0) * PAGE + lane
        for slot in range(PAGE):
            found = (table == (p.c * PAGE + slot).astype(jnp.float32)) & (lane < PAGE)
            to_ref[slot] = jnp.sum(jnp.where(found, page, 0))

    def leftover():
        for slot in range(8, 16, 2):
            mates(ck, cv, slot + 1 - p.core)
        for group in range(4):
            @pl.when(group > p.z)
            def _():
                stretch_mates(group, 0)
                stretch_mates(group, 1)
        for copy in outs:
            copy.start()
        sources()

    events = {
        1: first_stretch,
        2: far_stretch,
        3: near_stretch_y,
        4: far_stretch_y,
        6: own_cached,
        8: near_cached,
        10: wt.forward,
        11: near_cached_y,
        12: more_cached_y,
        15: far_cached,
        18: far_cached_y,
        23: leftover,
    }
    half = UNIT // 2
    first = lax.rem((p.z + 1) // 2, 2)

    def step(u, carry):
        for at, event in events.items():
            pl.when(u == at)(event)
        is_stretch = u < 2 * p.z + 2
        turn = jnp.where(u <= p.z, 0, 1)
        behind = jnp.maximum(p.z - u + turn * (p.z + 1), 0)
        pair = lax.rem(p.y + turn, 2)
        own_start = 2 * p.z + 2
        inside = p.z <= 1
        in_own = inside & (u >= own_start) & (u < own_start + 8)
        in_late = jnp.where(inside, (u >= 12) & (u < 20), u >= 8)
        late = jnp.maximum(u - 8, 0)
        other = jnp.maximum(u - 12, 0)
        mine = jnp.maximum(u - own_start, 0)
        group = jnp.where(in_own, first, jnp.where(inside | (late // 8 == 1), 1 - first, first))
        column = jnp.where(in_own, mine // 4, jnp.where(inside, other // 4, lax.rem(late // 4, 2)))
        within = lax.rem(jnp.where(in_own, mine, late), 4)
        y = lax.rem(p.y + column, 2)
        core = lax.rem(p.core + within // 2, 2)
        slot = lax.rem(group * 4 + y * 2 + core, 16)

        @pl.when(is_stretch)
        def _():
            stretch_mates(behind, pair)

        @pl.when(jnp.logical_not(is_stretch) & (in_own | in_late) & (core != p.core) & (lax.rem(within, 2) == 0))
        def _():
            mates(ck, cv, slot)

        def new_pair():
            pieces = [sbuf[behind * 4 + pair * 2 + i, 0:ROWS, :] for i in range(2)]
            both = jnp.concatenate(pieces, axis=0)
            return both[:, :D_HEAD], both[:, D_HEAD:]

        @pl.when(is_stretch & (behind == p.z))
        def _():
            k, v = new_pair()
            token = lax.broadcasted_iota(jnp.int32, (QROWS, half), 0) % ROWS
            ahead = lax.broadcasted_iota(jnp.int32, (QROWS, half), 1)
            allowed = ahead + pair * half <= token + lax.rem(p.c, 4) * ROWS
            attend(qs[...], k, v, m_ref, l_ref, a_ref, slice(None), allowed)

        @pl.when(is_stretch & (behind != p.z))
        def _():
            k, v = new_pair()
            attend(qs[...], k, v, m_ref, l_ref, a_ref, slice(None))

        @pl.when(jnp.logical_not(is_stretch) & (in_own | in_late))
        def _():
            keys = pl.ds(pl.multiple_of(slot * UNIT + lax.rem(within, 2) * half, half), half)
            attend(qs[...], kbuf[keys, :], vbuf[keys, :], m_ref, l_ref, a_ref, slice(None))

        return carry

    lax.fori_loop(0, 24, step, 0)

    for copy in outs:
        copy.wait()
    wown.wait()
    for flow in (st, ck, cv, wt):
        flow.finish()


def finish_attend(
    len_ref, t_ref, q_ref, k_ref, v_ref, m_in, l_in, a_in, new_ref,
    o_ref, p_ref,
    kbuf, vbuf, m_ref, l_ref, a_ref, qs, sem, ksem, vsem, psem,
):
    more = len_ref[0] - 8 * CSH
    whole = more // UNIT
    state = [
        pltpu.make_async_copy(src, dst, sem.at[i])
        for i, (src, dst) in enumerate(((q_ref, qs), (m_in, m_ref), (l_in, l_ref), (a_in, a_ref)))
    ]

    def fetch(u):
        keys = pl.ds(pl.multiple_of(u * UNIT, UNIT), UNIT)
        return (
            pltpu.make_async_copy(k_ref.at[keys], kbuf.at[keys], ksem.at[u]),
            pltpu.make_async_copy(v_ref.at[keys], vbuf.at[keys], vsem.at[u]),
        )

    for copy in (*state[:2], *fetch(0), *state[2:]):
        copy.start()
    for u in range(1, 8):
        for copy in fetch(u):
            copy.start()

    def page(source, slot):
        rows = pl.ds(pl.multiple_of(lax.rem(source, PAGE) * PAGE, PAGE), PAGE)
        return pltpu.make_async_copy(new_ref.at[source // PAGE, rows], p_ref.at[slot], psem.at[slot])

    for slot in range(PAGE):
        page(t_ref[slot], slot).start()
    for copy in state:
        copy.wait()

    def step(u, allowed):
        for copy in fetch(u):
            copy.wait()
        keys = pl.ds(pl.multiple_of(u * UNIT, UNIT), UNIT)
        attend(qs[...], kbuf[keys, :], vbuf[keys, :], m_ref, l_ref, a_ref, slice(None), allowed)

    def whole_step(u, carry):
        step(u, None)
        return carry

    lax.fori_loop(0, whole, whole_step, 0)

    @pl.when(more - whole * UNIT > 0)
    def _():
        place = lax.broadcasted_iota(jnp.int32, (QROWS, UNIT), 1)
        step(whole, place < more - whole * UNIT)

    def unused(u, carry):
        for copy in fetch(u):
            copy.wait()
        return carry

    lax.fori_loop((more + UNIT - 1) // UNIT, 8, unused, 0)

    for h in range(GROUP):
        rows = pl.ds(h * ROWS, ROWS)
        total = jnp.sum(l_ref[rows, :], axis=1, keepdims=True)
        o_ref[:, pl.ds(h * D_HEAD, D_HEAD)] = (a_ref[rows, :] / total).astype(jnp.bfloat16)
    for slot in range(PAGE):
        page(0, slot).wait()


def project(
    att_ref, w_ref, o_ref,
    x, w, pb, qb, keep, yb, ob,
    asend, arecv, send, recv, psend, precv, osend, orecv, local,
):
    p = Place()
    ac = Across()
    x_others = ((ac.rp, ac.xp), (ac.rm, ac.xm), (ac.r2, ac.x2))
    ctx_others = [lax.rem(p.c + d, N_CTX) for d in range(1, N_CTX)]
    wcopy = pltpu.make_async_copy(w_ref, w, local.at[0])
    wcopy.start()

    def rows_of(r, j):
        return pl.ds(pl.multiple_of((r + 4 * j) * 32, 32), 32)

    def cols_of(s, n):
        return pl.ds(pl.multiple_of(s * n, n), n)

    mine = [
        pltpu.make_async_copy(
            att_ref.at[rows_of(ac.x, j)], x.at[p.c, j, :, cols_of(ac.x, 1024)], local.at[1 + j]
        )
        for j in range(2)
    ]
    for copy in mine:
        copy.start()
    greet([{"tp": s} for s in (ac.xp, ac.xm, ac.x2, ac.yh)] + [{"ctx": s} for s in ctx_others])

    def swap(j, r, dest, source, index):
        return pltpu.make_async_remote_copy(
            src_ref=att_ref.at[rows_of(r, j)],
            dst_ref=x.at[p.c, j, :, cols_of(source, 1024)],
            send_sem=asend.at[j, index],
            recv_sem=arecv.at[j, source],
            device_id={"tp": dest},
            device_id_type=pl.DeviceIdType.MESH,
        )

    for j in (1, 0):
        for index, (r, dest) in enumerate(x_others):
            swap(j, r, dest, ac.x, index).start()

    def half(j):
        def view(slot, part):
            cols = pl.ds(0, 4096) if part is None else pl.ds(part * 2048, 2048)
            return x.at[slot, j, :, cols]
        return view

    fz = Flow(p, half(0), send.at[0], recv.at[0], "y")
    fy = Flow(p, half(1), send.at[1], recv.at[1], "y")
    for j, flow in ((1, fy), (0, fz)):
        mine[j].wait()
        for r, dest in x_others:
            swap(j, r, dest, r, 0).wait_recv()
        flow.own()

    def give(dest, source, index):
        return pltpu.make_async_remote_copy(
            src_ref=yb.at[dest],
            dst_ref=ob.at[:, cols_of(source, 512)],
            send_sem=osend.at[index],
            recv_sem=orecv.at[source],
            device_id={"ctx": dest},
            device_id_type=pl.DeviceIdType.MESH,
        )

    def cross(group):
        slots = pl.ds(group * 4, 4)
        return pltpu.make_async_remote_copy(
            src_ref=pb.at[slots],
            dst_ref=qb.at[slots],
            send_sem=psend.at[group],
            recv_sem=precv.at[group],
            device_id={"tp": ac.yh},
            device_id_type=pl.DeviceIdType.MESH,
        )

    def multiply(group):
        slots = pl.ds(group * 4, 4)
        for y in range(2):
            for flow in (fz, fy):
                flow.wait(group * 4 + y * 2 + 1 - p.core)

        def part(j):
            def step(k, total):
                a = x[slots, j, :, cols_of(k, 1024)].reshape(128, 1024)
                return total + jnp.dot(a, w[k], preferred_element_type=jnp.float32)

            return lax.fori_loop(0, 4, step, jnp.zeros((128, 512), jnp.float32)).reshape(4, 32, 512)

        pb[slots] = part(1 - ac.h).astype(jnp.bfloat16)
        cross(group).start()
        keep[slots] = part(ac.h)

    def combine(group):
        slots = pl.ds(group * 4, 4)
        cross(group).wait_recv()
        yb[slots] = (keep[slots] + qb[slots].astype(jnp.float32)).astype(jnp.bfloat16)
        for i in range(4):
            dest = group * 4 + i

            @pl.when(dest != p.c)
            def _():
                give(dest, p.c, dest).start()

    g0, gm, gp, g2 = p.z, p.zm // 4, p.zp // 4, p.z2 // 4
    both = (fy, fz)
    for flow in both:
        flow.y(p.cy)
    for flow in both:
        flow.from_zm(p.zm)
        flow.from_zp(p.zp)
    wcopy.wait()
    multiply(g0)
    for flow in both:
        flow.from_zm(p.zmy)
        flow.from_zp(p.zpy)
    combine(g0)
    ob[:, cols_of(p.c, 512)] = yb[p.c]
    multiply(gm)
    for flow in both:
        flow.from_z2(p.z2)
    multiply(gp)
    combine(gm)
    for flow in both:
        flow.from_z2(p.z2y)
    multiply(g2)
    combine(gp)
    combine(g2)

    for s in ctx_others:
        give(s, s, s).wait_recv()
    o_ref[...] = ob[...]
    for j in range(2):
        for index, (r, dest) in enumerate(x_others):
            swap(j, r, dest, ac.x, index).wait_send()
    for s in ctx_others:
        give(s, p.c, s).wait_send()
    for group in range(4):
        cross(group).wait_send()
    for flow in (fz, fy):
        flow.finish()


VMEM = pl.BlockSpec(memory_space=pltpu.VMEM)
ANY = pl.BlockSpec(memory_space=pl.ANY)
SMEM = pl.BlockSpec(memory_space=pltpu.SMEM)


def local(
    queries,
    stretch_keys,
    stretch_values,
    cache_keys,
    cache_values,
    cached_len,
    page_table,
    out_weight,
):
    bf16, f32 = jnp.bfloat16, jnp.float32
    state = jax.ShapeDtypeStruct((QROWS, D_HEAD), f32)
    m, l, a, heads, more_k, more_v, new, sources, weight = pl.pallas_call(
        gather_attend,
        name="gather_attend",
        out_shape=(
            state,
            state,
            state,
            jax.ShapeDtypeStruct((QROWS, D_HEAD), bf16),
            jax.ShapeDtypeStruct((8 * CSH, D_HEAD), bf16),
            jax.ShapeDtypeStruct((8 * CSH, D_HEAD), bf16),
            jax.ShapeDtypeStruct((N_CTX, SROWS, 2 * D_HEAD), bf16),
            jax.ShapeDtypeStruct((PAGE,), jnp.int32),
            jax.ShapeDtypeStruct((4, 1024, 512), bf16),
        ),
        in_specs=[VMEM, ANY, ANY, ANY, ANY, VMEM, ANY],
        out_specs=(VMEM, VMEM, VMEM, VMEM, ANY, ANY, ANY, SMEM, ANY),
        scratch_shapes=[
            pltpu.VMEM((BASE, D_HEAD), bf16),
            pltpu.VMEM((BASE, D_HEAD), bf16),
            pltpu.VMEM((N_CTX, SROWS, 2 * D_HEAD), bf16),
            pltpu.SemaphoreType.DMA((3, 20)),
            pltpu.SemaphoreType.DMA((3, 32)),
            pltpu.SemaphoreType.DMA((8,)),
            pltpu.SemaphoreType.DMA((N_TP,)),
            pltpu.SemaphoreType.DMA((5,)),
        ],
        compiler_params=pltpu.CompilerParams(
            collective_id=1, has_side_effects=True, vmem_limit_bytes=62 * MIB
        ),
        cost_estimate=pl.CostEstimate(
            flops=4 * QROWS * 10 * UNIT * D_HEAD, bytes_accessed=20 * MIB, transcendentals=QROWS * 10 * UNIT
        ),
    )(queries, stretch_keys, stretch_values, cache_keys, cache_values, page_table.reshape(1, PAGE), out_weight)

    attended, pages = pl.pallas_call(
        finish_attend,
        name="finish_attend",
        out_shape=(
            jax.ShapeDtypeStruct((ROWS, GROUP * D_HEAD), bf16),
            jax.ShapeDtypeStruct((PAGE, PAGE, 2 * D_HEAD), bf16),
        ),
        in_specs=[SMEM] * 2 + [ANY] * 7,
        out_specs=(VMEM, ANY),
        scratch_shapes=[
            pltpu.VMEM((8 * CSH, D_HEAD), bf16),
            pltpu.VMEM((8 * CSH, D_HEAD), bf16),
            pltpu.VMEM((QROWS, D_HEAD), f32),
            pltpu.VMEM((QROWS, D_HEAD), f32),
            pltpu.VMEM((QROWS, D_HEAD), f32),
            pltpu.VMEM((QROWS, D_HEAD), bf16),
            pltpu.SemaphoreType.DMA((4,)),
            pltpu.SemaphoreType.DMA((8,)),
            pltpu.SemaphoreType.DMA((8,)),
            pltpu.SemaphoreType.DMA((PAGE,)),
        ],
        compiler_params=pltpu.CompilerParams(vmem_limit_bytes=60 * MIB),
        cost_estimate=pl.CostEstimate(
            flops=4 * QROWS * 4 * UNIT * D_HEAD, bytes_accessed=8 * MIB, transcendentals=QROWS * 4 * UNIT
        ),
    )(cached_len, sources, heads, more_k, more_v, m, l, a, new)

    projected = pl.pallas_call(
        project,
        name="project",
        out_shape=jax.ShapeDtypeStruct((32, 8192), bf16),
        in_specs=[ANY, ANY],
        out_specs=VMEM,
        scratch_shapes=[
            pltpu.VMEM((N_CTX, 2, 32, 4096), bf16),
            pltpu.VMEM((4, 1024, 512), bf16),
            pltpu.VMEM((N_CTX, 32, 512), bf16),
            pltpu.VMEM((N_CTX, 32, 512), bf16),
            pltpu.VMEM((N_CTX, 32, 512), f32),
            pltpu.VMEM((N_CTX, 32, 512), bf16),
            pltpu.VMEM((32, 8192), bf16),
            pltpu.SemaphoreType.DMA((2, 4)),
            pltpu.SemaphoreType.DMA((2, 4)),
            pltpu.SemaphoreType.DMA((2, 20)),
            pltpu.SemaphoreType.DMA((2, 32)),
            pltpu.SemaphoreType.DMA((4,)),
            pltpu.SemaphoreType.DMA((4,)),
            pltpu.SemaphoreType.DMA((N_CTX,)),
            pltpu.SemaphoreType.DMA((N_CTX,)),
            pltpu.SemaphoreType.DMA((3,)),
        ],
        compiler_params=pltpu.CompilerParams(
            collective_id=2, has_side_effects=True, vmem_limit_bytes=62 * MIB
        ),
        cost_estimate=pl.CostEstimate(
            flops=2 * 512 * 512 * 8192, bytes_accessed=20 * MIB, transcendentals=0
        ),
    )(attended, weight)

    paged_kv = pages.reshape(PAGE, PAGE, 2, D_HEAD)
    return (projected, paged_kv)


def solution(mesh):
    return jax.shard_map(
        local,
        mesh=mesh,
        in_specs=(
            P("ctx", "tp"),
            P("ctx", "tp"),
            P("ctx", "tp"),
            P("ctx", "tp"),
            P("ctx", "tp"),
            P(),
            P("ctx"),
            P("tp", "ctx"),
        ),
        out_specs=(P(("ctx", "tp"), None), P("ctx", None, None, "tp")),
        check_vma=False,
    )
```

```python
import functools
import math

import jax
import jax.numpy as jnp
from jax import lax
from jax.experimental import pallas as pl
from jax.experimental.pallas import tpu as pltpu
from jax.sharding import PartitionSpec as P

HEADS = 64
KV_HEADS = 8
D_HEAD = 128
PAGE = 16
GROUP = HEADS // KV_HEADS
ROWS = 256
QROWS = ROWS * GROUP
CSH = 1024
N_CTX = 16
N_TP = 8
UNIT = 1024
BASE = N_CTX * CSH
SROWS = ROWS + 16
TILE = 1024
EXPC = D_HEAD ** (-0.5) * math.log2(math.e)
MIB = 2**20


class Place:
    def __init__(self):
        c = lax.axis_index("ctx")
        self.c = c
        self.z = c // 4
        self.y = lax.rem(c // 2, 2)
        self.core = lax.rem(c, 2)
        self.zp = lax.rem(c + 4, 16)
        self.zm = lax.rem(c + 12, 16)
        self.z2 = lax.rem(c + 8, 16)
        self.dy = 2 - 4 * self.y
        self.dm = 1 - 2 * self.core
        self.yp = c + self.dy
        self.mate = c + self.dm
        self.cy, self.zmy, self.zpy, self.z2y = (
            slot + self.dy for slot in (c, self.zm, self.zp, self.z2)
        )


class Flow:
    def __init__(self, place, view, send, recv, kind, far="halves"):
        self.p, self.view, self.ss, self.rs = place, view, send, recv
        self.kind, self.far = kind, far
        self.sent = []

    def _copy(self, slot, part, dest, index):
        ref = self.view(slot, part)
        return pltpu.make_async_remote_copy(
            src_ref=ref,
            dst_ref=ref,
            send_sem=self.ss.at[index],
            recv_sem=self.rs.at[slot + (16 if part == 1 else 0)],
            device_id={"ctx": dest},
            device_id_type=pl.DeviceIdType.MESH,
        )

    def send(self, slot, part, dest):
        item = (slot, part, dest, len(self.sent))
        self.sent.append(item)
        self._copy(*item).start()

    def wait(self, slot, part=None):
        self._copy(slot, part, self.p.mate, 0).wait_recv()

    def finish(self):
        for item in self.sent:
            self._copy(*item).wait_send()

    def _along_z(self, slot):
        self.send(slot, None, self.p.zp)
        self.send(slot, None, self.p.zm)
        if self.far == "direct":
            self.send(slot, None, self.p.z2)

    def own(self):
        p = self.p
        if self.kind == "y":
            self.send(p.c, None, p.yp)
        self._along_z(p.c)
        if self.kind == "z":
            self.send(p.c, None, p.yp)
        self.send(p.c, None, p.mate)

    def _down(self, slot):
        if self.kind == "z":
            self.send(slot, None, self.p.yp)
        self.send(slot, None, self.p.mate)

    def y(self, slot):
        self.wait(slot)
        if self.kind == "y":
            self._along_z(slot)
        self.send(slot, None, self.p.mate)

    def from_zm(self, slot):
        self.wait(slot)
        if self.far == "halves":
            self.send(slot, 0, self.p.zp)
        self._down(slot)

    def from_zp(self, slot):
        self.wait(slot)
        if self.far == "halves":
            self.send(slot, 1, self.p.zm)
        self._down(slot)

    def from_z2(self, slot):
        if self.far == "halves":
            self.wait(slot, 0)
            self.wait(slot, 1)
        else:
            self.wait(slot)
        self._down(slot)


class Across:
    def __init__(self):
        t = lax.axis_index("tp")
        x = lax.rem(t, 4)
        self.t, self.x, self.h = t, x, t // 4
        self.rp, self.rm, self.r2 = (lax.rem(x + d, 4) for d in (1, 3, 2))
        self.xp, self.xm, self.x2 = (t - x + r for r in (self.rp, self.rm, self.r2))
        self.yh = lax.rem(t + 4, N_TP)


class Weight:
    def __init__(self, place, own, buf, send, recv):
        self.p, self.own, self.buf, self.ss, self.rs = place, own, buf, send, recv
        self.sent = []

    def _copy(self, src, slot, part, dest, index):
        rows = pl.ds(0, 1024) if part is None else pl.ds(part * 512, 512)
        dst = self.buf.at[slot, rows]
        return pltpu.make_async_remote_copy(
            src_ref=dst if src is None else src,
            dst_ref=dst,
            send_sem=self.ss.at[index],
            recv_sem=self.rs.at[slot + (4 if part == 1 else 0)],
            device_id={"tp": dest},
            device_id_type=pl.DeviceIdType.MESH,
        )

    def send(self, src, slot, part, dest):
        item = (src, slot, part, dest, len(self.sent))
        self.sent.append(item)
        self._copy(*item).start()

    def wait(self, slot, part=None):
        self._copy(None, slot, part, self.p.yh, 0).wait_recv()

    def start(self):
        self.send(self.own, self.p.x, None, self.p.xp)
        self.send(self.own, self.p.x, None, self.p.xm)

    def forward(self):
        self.wait(self.p.rm)
        self.send(None, self.p.rm, 0, self.p.xp)
        self.wait(self.p.rp)
        self.send(None, self.p.rp, 1, self.p.xm)

    def finish(self):
        self.wait(self.p.r2, 0)
        self.wait(self.p.r2, 1)
        for item in self.sent:
            self._copy(*item).wait_send()


def greet(partners):
    barrier = pltpu.get_barrier_semaphore()
    for partner in partners:
        pl.semaphore_signal(
            barrier, inc=1, device_id=partner, device_id_type=pl.DeviceIdType.MESH
        )
    pl.semaphore_wait(barrier, len(partners))


def attend(q, k, v, m_ref, l_ref, a_ref, rows, allowed=None):
    s = lax.dot_general(q, k, (((1,), (1,)), ((), ())), preferred_element_type=jnp.float32)
    if allowed is not None:
        s = jnp.where(allowed, s, -1e30)
    m = m_ref[rows, :]
    top = jnp.maximum(m, jnp.max(s, axis=1, keepdims=True))
    m_ref[rows, :] = top
    factor = jnp.exp2((m - top) * EXPC)
    w = jnp.exp2((s - jnp.tile(top, (1, s.shape[1] // 128))) * EXPC)
    part = functools.reduce(jnp.add, [w[:, i : i + 128] for i in range(0, w.shape[1], 128)])
    l_ref[rows, :] = l_ref[rows, :] * factor + part
    a_ref[rows, :] = a_ref[rows, :] * factor + jnp.dot(
        w.astype(jnp.bfloat16), v, preferred_element_type=jnp.float32
    )


def gather_attend(
    q_ref, sk_ref, sv_ref, ck_ref, cv_ref, t_ref, w_ref,
    m_ref, l_ref, a_ref, qs, ko_ref, vo_ref, so_ref, to_ref, wo_ref,
    kbuf, vbuf, sbuf, send, recv, wsend, wrecv, local,
):
    p = Place()
    across = Across()
    wt = Weight(across, w_ref, wo_ref, wsend, wrecv)

    def cached(buf):
        def view(slot, part):
            rows = CSH if part is None else CSH // 2
            first = slot * CSH + (CSH // 2 if part == 1 else 0)
            return buf.at[pl.ds(pl.multiple_of(first, CSH // 2), rows)]
        return view

    st = Flow(p, lambda slot, part: sbuf.at[slot], send.at[0], recv.at[0], "y", "direct")
    ck = Flow(p, cached(kbuf), send.at[1], recv.at[1], "z")
    cv = Flow(p, cached(vbuf), send.at[2], recv.at[2], "y")

    own = [
        pltpu.make_async_copy(sk_ref, sbuf.at[p.c, pl.ds(0, ROWS), pl.ds(0, D_HEAD)], local.at[0]),
        pltpu.make_async_copy(
            sv_ref, sbuf.at[p.c, pl.ds(0, ROWS), pl.ds(D_HEAD, D_HEAD)], local.at[1]
        ),
        pltpu.make_async_copy(ck_ref, ck.view(p.c, None), local.at[2]),
        pltpu.make_async_copy(cv_ref, cv.view(p.c, None), local.at[3]),
    ]
    for copy in own:
        copy.start()
    wown = pltpu.make_async_copy(w_ref, wo_ref.at[across.x], local.at[4])
    wown.start()
    sbuf[p.c, ROWS:SROWS, :] = jnp.zeros((16, 2 * D_HEAD), jnp.bfloat16)
    entries = jnp.broadcast_to(t_ref[...].astype(jnp.float32), (16, PAGE))
    sbuf[p.c, ROWS:SROWS, 0:PAGE] = entries.astype(jnp.bfloat16)
    greet(
        [{"ctx": x} for x in (p.zp, p.zm, p.z2, p.yp, p.mate)]
        + [{"tp": x} for x in (across.xp, across.xm)]
    )
    own[0].wait()
    own[1].wait()
    st.own()
    wt.start()

    for h in range(GROUP):
        qs[pl.ds(h * ROWS, ROWS), :] = q_ref[:, pl.ds(h * D_HEAD, D_HEAD)]
    m_ref[...] = jnp.full_like(m_ref, -1e30)
    l_ref[...] = jnp.zeros_like(l_ref)
    a_ref[...] = jnp.zeros_like(a_ref)

    def mates(flow_k, flow_v, slot):
        flow_k.wait(slot)
        flow_v.wait(slot)

    def stretch_mates(group, y):
        st.wait(group * 4 + y * 2 + 1 - p.core)

    def first_stretch():
        st.y(p.cy)
        own[2].wait()
        own[3].wait()
        ck.own()
        cv.own()
        st.from_zm(p.zm)
        st.from_zp(p.zp)

    def far_stretch():
        st.from_z2(p.z2)

    def near_stretch_y():
        st.from_zm(p.zmy)
        st.from_zp(p.zpy)

    def far_stretch_y():
        st.from_z2(p.z2y)

    def own_cached():
        cv.y(p.cy)
        ck.y(p.cy)

    def near_cached():
        for flow in (ck, cv):
            flow.from_zm(p.zm)
            flow.from_zp(p.zp)

    def far_cached():
        ck.from_z2(p.z2)
        cv.from_z2(p.z2)

    def near_cached_y():
        cv.from_zm(p.zmy)
        cv.from_zp(p.zpy)

    def more_cached_y():
        ck.y(p.zmy)
        ck.y(p.zpy)

    def far_cached_y():
        ck.y(p.z2y)
        cv.from_z2(p.z2y)

    outs = [
        pltpu.make_async_copy(kbuf.at[pl.ds(8 * CSH, 8 * CSH)], ko_ref, local.at[0]),
        pltpu.make_async_copy(vbuf.at[pl.ds(8 * CSH, 8 * CSH)], vo_ref, local.at[1]),
        pltpu.make_async_copy(sbuf, so_ref, local.at[2]),
    ]

    def sources():
        table = sbuf[:, ROWS:SROWS, 0:128][:, 0, :].astype(jnp.float32)
        lane = lax.broadcasted_iota(jnp.int32, (N_CTX, 128), 1)
        page = lax.broadcasted_iota(jnp.int32, (N_CTX, 128), 0) * PAGE + lane
        for slot in range(PAGE):
            found = (table == (p.c * PAGE + slot).astype(jnp.float32)) & (lane < PAGE)
            to_ref[slot] = jnp.sum(jnp.where(found, page, 0))

    def leftover():
        for slot in range(8, 16, 2):
            mates(ck, cv, slot + 1 - p.core)
        for group in range(4):
            @pl.when(group > p.z)
            def _():
                stretch_mates(group, 0)
                stretch_mates(group, 1)
        for copy in outs:
            copy.start()
        sources()

    events = {
        1: first_stretch,
        2: far_stretch,
        3: near_stretch_y,
        4: far_stretch_y,
        5: own_cached,
        8: near_cached,
        10: wt.forward,
        11: near_cached_y,
        12: more_cached_y,
        14: far_cached,
        17: far_cached_y,
        22: leftover,
    }
    half = UNIT // 2
    first = lax.rem((p.z + 1) // 2, 2)

    def step(u, carry):
        for at, event in events.items():
            pl.when(u == at)(event)
        is_stretch = u < 2 * p.z + 2
        turn = jnp.where(u <= p.z, 0, 1)
        behind = jnp.maximum(p.z - u + turn * (p.z + 1), 0)
        pair = lax.rem(p.y + turn, 2)
        own_start = 2 * p.z + 2
        inside = p.z <= 1
        in_own = inside & (u >= own_start) & (u < own_start + 8)
        in_late = jnp.where(inside, (u >= 12) & (u < 20), u >= 8)
        late = jnp.maximum(u - 8, 0)
        other = jnp.maximum(u - 12, 0)
        mine = jnp.maximum(u - own_start, 0)
        group = jnp.where(in_own, first, jnp.where(inside | (late // 8 == 1), 1 - first, first))
        column = jnp.where(in_own, mine // 4, jnp.where(inside, other // 4, lax.rem(late // 4, 2)))
        within = lax.rem(jnp.where(in_own, mine, late), 4)
        y = lax.rem(p.y + column, 2)
        core = lax.rem(p.core + within // 2, 2)
        slot = lax.rem(group * 4 + y * 2 + core, 16)

        @pl.when(is_stretch)
        def _():
            stretch_mates(behind, pair)

        @pl.when(jnp.logical_not(is_stretch) & (in_own | in_late) & (core != p.core) & (lax.rem(within, 2) == 0))
        def _():
            mates(ck, cv, slot)

        def new_pair():
            pieces = [sbuf[behind * 4 + pair * 2 + i, 0:ROWS, :] for i in range(2)]
            both = jnp.concatenate(pieces, axis=0)
            return both[:, :D_HEAD], both[:, D_HEAD:]

        @pl.when(is_stretch & (behind == p.z))
        def _():
            k, v = new_pair()
            token = lax.broadcasted_iota(jnp.int32, (QROWS, half), 0) % ROWS
            ahead = lax.broadcasted_iota(jnp.int32, (QROWS, half), 1)
            allowed = ahead + pair * half <= token + lax.rem(p.c, 4) * ROWS
            attend(qs[...], k, v, m_ref, l_ref, a_ref, slice(None), allowed)

        @pl.when(is_stretch & (behind != p.z))
        def _():
            k, v = new_pair()
            attend(qs[...], k, v, m_ref, l_ref, a_ref, slice(None))

        @pl.when(jnp.logical_not(is_stretch) & (in_own | in_late))
        def _():
            keys = pl.ds(pl.multiple_of(slot * UNIT + lax.rem(within, 2) * half, half), half)
            attend(qs[...], kbuf[keys, :], vbuf[keys, :], m_ref, l_ref, a_ref, slice(None))

        return carry

    lax.fori_loop(0, 24, step, 0)

    for copy in outs:
        copy.wait()
    wown.wait()
    for flow in (st, ck, cv, wt):
        flow.finish()


def finish_attend(
    len_ref, t_ref, q_ref, k_ref, v_ref, m_in, l_in, a_in, new_ref,
    o_ref, p_ref,
    kbuf, vbuf, m_ref, l_ref, a_ref, qs, sem, ksem, vsem, psem,
):
    more = len_ref[0] - 8 * CSH
    whole = more // UNIT
    state = [
        pltpu.make_async_copy(src, dst, sem.at[i])
        for i, (src, dst) in enumerate(((q_ref, qs), (m_in, m_ref), (l_in, l_ref), (a_in, a_ref)))
    ]

    def fetch(u):
        keys = pl.ds(pl.multiple_of(u * UNIT, UNIT), UNIT)
        return (
            pltpu.make_async_copy(k_ref.at[keys], kbuf.at[keys], ksem.at[u]),
            pltpu.make_async_copy(v_ref.at[keys], vbuf.at[keys], vsem.at[u]),
        )

    for copy in (*state[:2], *fetch(0), *state[2:]):
        copy.start()
    for u in range(1, 8):
        for copy in fetch(u):
            copy.start()

    def page(source, slot):
        rows = pl.ds(pl.multiple_of(lax.rem(source, PAGE) * PAGE, PAGE), PAGE)
        return pltpu.make_async_copy(new_ref.at[source // PAGE, rows], p_ref.at[slot], psem.at[slot])

    for slot in range(PAGE):
        page(t_ref[slot], slot).start()
    for copy in state:
        copy.wait()

    def step(u, allowed):
        for copy in fetch(u):
            copy.wait()
        keys = pl.ds(pl.multiple_of(u * UNIT, UNIT), UNIT)
        attend(qs[...], kbuf[keys, :], vbuf[keys, :], m_ref, l_ref, a_ref, slice(None), allowed)

    def whole_step(u, carry):
        step(u, None)
        return carry

    lax.fori_loop(0, whole, whole_step, 0)

    @pl.when(more - whole * UNIT > 0)
    def _():
        place = lax.broadcasted_iota(jnp.int32, (QROWS, UNIT), 1)
        step(whole, place < more - whole * UNIT)

    def unused(u, carry):
        for copy in fetch(u):
            copy.wait()
        return carry

    lax.fori_loop((more + UNIT - 1) // UNIT, 8, unused, 0)

    for h in range(GROUP):
        rows = pl.ds(h * ROWS, ROWS)
        total = jnp.sum(l_ref[rows, :], axis=1, keepdims=True)
        o_ref[:, pl.ds(h * D_HEAD, D_HEAD)] = (a_ref[rows, :] / total).astype(jnp.bfloat16)
    for slot in range(PAGE):
        page(0, slot).wait()


def project(
    att_ref, w_ref, o_ref,
    x, w, pb, qb, keep, yb, ob,
    asend, arecv, send, recv, psend, precv, osend, orecv, local,
):
    p = Place()
    ac = Across()
    x_others = ((ac.rp, ac.xp), (ac.rm, ac.xm), (ac.r2, ac.x2))
    ctx_others = [lax.rem(p.c + d, N_CTX) for d in range(1, N_CTX)]
    wcopy = pltpu.make_async_copy(w_ref, w, local.at[0])
    wcopy.start()

    def rows_of(r, j):
        return pl.ds(pl.multiple_of((r + 4 * j) * 32, 32), 32)

    def cols_of(s, n):
        return pl.ds(pl.multiple_of(s * n, n), n)

    mine = [
        pltpu.make_async_copy(
            att_ref.at[rows_of(ac.x, j)], x.at[p.c, j, :, cols_of(ac.x, 1024)], local.at[1 + j]
        )
        for j in range(2)
    ]
    for copy in mine:
        copy.start()
    greet([{"tp": s} for s in (ac.xp, ac.xm, ac.x2, ac.yh)] + [{"ctx": s} for s in ctx_others])

    def swap(j, r, dest, source, index):
        return pltpu.make_async_remote_copy(
            src_ref=att_ref.at[rows_of(r, j)],
            dst_ref=x.at[p.c, j, :, cols_of(source, 1024)],
            send_sem=asend.at[j, index],
            recv_sem=arecv.at[j, source],
            device_id={"tp": dest},
            device_id_type=pl.DeviceIdType.MESH,
        )

    for j in (1, 0):
        for index, (r, dest) in enumerate(x_others):
            swap(j, r, dest, ac.x, index).start()

    def half(j):
        def view(slot, part):
            cols = pl.ds(0, 4096) if part is None else pl.ds(part * 2048, 2048)
            return x.at[slot, j, :, cols]
        return view

    fz = Flow(p, half(0), send.at[0], recv.at[0], "y")
    fy = Flow(p, half(1), send.at[1], recv.at[1], "y")
    for j, flow in ((1, fy), (0, fz)):
        mine[j].wait()
        for r, dest in x_others:
            swap(j, r, dest, r, 0).wait_recv()
        flow.own()

    def give(dest, source, index):
        return pltpu.make_async_remote_copy(
            src_ref=yb.at[dest],
            dst_ref=ob.at[:, cols_of(source, 512)],
            send_sem=osend.at[index],
            recv_sem=orecv.at[source],
            device_id={"ctx": dest},
            device_id_type=pl.DeviceIdType.MESH,
        )

    def cross(group):
        slots = pl.ds(group * 4, 4)
        return pltpu.make_async_remote_copy(
            src_ref=pb.at[slots],
            dst_ref=qb.at[slots],
            send_sem=psend.at[group],
            recv_sem=precv.at[group],
            device_id={"tp": ac.yh},
            device_id_type=pl.DeviceIdType.MESH,
        )

    def multiply(group):
        slots = pl.ds(group * 4, 4)
        for y in range(2):
            for flow in (fz, fy):
                flow.wait(group * 4 + y * 2 + 1 - p.core)

        def part(j):
            def step(k, total):
                a = x[slots, j, :, cols_of(k, 1024)].reshape(128, 1024)
                return total + jnp.dot(a, w[k], preferred_element_type=jnp.float32)

            return lax.fori_loop(0, 4, step, jnp.zeros((128, 512), jnp.float32)).reshape(4, 32, 512)

        pb[slots] = part(1 - ac.h).astype(jnp.bfloat16)
        cross(group).start()
        keep[slots] = part(ac.h)

    def combine(group):
        slots = pl.ds(group * 4, 4)
        cross(group).wait_recv()
        yb[slots] = (keep[slots] + qb[slots].astype(jnp.float32)).astype(jnp.bfloat16)
        for i in range(4):
            dest = group * 4 + i

            @pl.when(dest != p.c)
            def _():
                give(dest, p.c, dest).start()

    g0, gm, gp, g2 = p.z, p.zm // 4, p.zp // 4, p.z2 // 4
    both = (fy, fz)
    for flow in both:
        flow.y(p.cy)
    for flow in both:
        flow.from_zm(p.zm)
        flow.from_zp(p.zp)
    wcopy.wait()
    multiply(g0)
    for flow in both:
        flow.from_zm(p.zmy)
        flow.from_zp(p.zpy)
    combine(g0)
    ob[:, cols_of(p.c, 512)] = yb[p.c]
    multiply(gm)
    for flow in both:
        flow.from_z2(p.z2)
    multiply(gp)
    combine(gm)
    for flow in both:
        flow.from_z2(p.z2y)
    multiply(g2)
    combine(gp)
    combine(g2)

    for s in ctx_others:
        give(s, s, s).wait_recv()
    o_ref[...] = ob[...]
    for j in range(2):
        for index, (r, dest) in enumerate(x_others):
            swap(j, r, dest, ac.x, index).wait_send()
    for s in ctx_others:
        give(s, p.c, s).wait_send()
    for group in range(4):
        cross(group).wait_send()
    for flow in (fz, fy):
        flow.finish()


VMEM = pl.BlockSpec(memory_space=pltpu.VMEM)
ANY = pl.BlockSpec(memory_space=pl.ANY)
SMEM = pl.BlockSpec(memory_space=pltpu.SMEM)


def local(
    queries,
    stretch_keys,
    stretch_values,
    cache_keys,
    cache_values,
    cached_len,
    page_table,
    out_weight,
):
    bf16, f32 = jnp.bfloat16, jnp.float32
    state = jax.ShapeDtypeStruct((QROWS, D_HEAD), f32)
    m, l, a, heads, more_k, more_v, new, sources, weight = pl.pallas_call(
        gather_attend,
        name="gather_attend",
        out_shape=(
            state,
            state,
            state,
            jax.ShapeDtypeStruct((QROWS, D_HEAD), bf16),
            jax.ShapeDtypeStruct((8 * CSH, D_HEAD), bf16),
            jax.ShapeDtypeStruct((8 * CSH, D_HEAD), bf16),
            jax.ShapeDtypeStruct((N_CTX, SROWS, 2 * D_HEAD), bf16),
            jax.ShapeDtypeStruct((PAGE,), jnp.int32),
            jax.ShapeDtypeStruct((4, 1024, 512), bf16),
        ),
        in_specs=[VMEM, ANY, ANY, ANY, ANY, VMEM, ANY],
        out_specs=(VMEM, VMEM, VMEM, VMEM, ANY, ANY, ANY, SMEM, ANY),
        scratch_shapes=[
            pltpu.VMEM((BASE, D_HEAD), bf16),
            pltpu.VMEM((BASE, D_HEAD), bf16),
            pltpu.VMEM((N_CTX, SROWS, 2 * D_HEAD), bf16),
            pltpu.SemaphoreType.DMA((3, 20)),
            pltpu.SemaphoreType.DMA((3, 32)),
            pltpu.SemaphoreType.DMA((8,)),
            pltpu.SemaphoreType.DMA((N_TP,)),
            pltpu.SemaphoreType.DMA((5,)),
        ],
        compiler_params=pltpu.CompilerParams(
            collective_id=1, has_side_effects=True, vmem_limit_bytes=62 * MIB
        ),
        cost_estimate=pl.CostEstimate(
            flops=4 * QROWS * 10 * UNIT * D_HEAD, bytes_accessed=20 * MIB, transcendentals=QROWS * 10 * UNIT
        ),
    )(queries, stretch_keys, stretch_values, cache_keys, cache_values, page_table.reshape(1, PAGE), out_weight)

    attended, pages = pl.pallas_call(
        finish_attend,
        name="finish_attend",
        out_shape=(
            jax.ShapeDtypeStruct((ROWS, GROUP * D_HEAD), bf16),
            jax.ShapeDtypeStruct((PAGE, PAGE, 2 * D_HEAD), bf16),
        ),
        in_specs=[SMEM] * 2 + [ANY] * 7,
        out_specs=(VMEM, ANY),
        scratch_shapes=[
            pltpu.VMEM((8 * CSH, D_HEAD), bf16),
            pltpu.VMEM((8 * CSH, D_HEAD), bf16),
            pltpu.VMEM((QROWS, D_HEAD), f32),
            pltpu.VMEM((QROWS, D_HEAD), f32),
            pltpu.VMEM((QROWS, D_HEAD), f32),
            pltpu.VMEM((QROWS, D_HEAD), bf16),
            pltpu.SemaphoreType.DMA((4,)),
            pltpu.SemaphoreType.DMA((8,)),
            pltpu.SemaphoreType.DMA((8,)),
            pltpu.SemaphoreType.DMA((PAGE,)),
        ],
        compiler_params=pltpu.CompilerParams(vmem_limit_bytes=60 * MIB),
        cost_estimate=pl.CostEstimate(
            flops=4 * QROWS * 4 * UNIT * D_HEAD, bytes_accessed=8 * MIB, transcendentals=QROWS * 4 * UNIT
        ),
    )(cached_len, sources, heads, more_k, more_v, m, l, a, new)

    projected = pl.pallas_call(
        project,
        name="project",
        out_shape=jax.ShapeDtypeStruct((32, 8192), bf16),
        in_specs=[ANY, ANY],
        out_specs=VMEM,
        scratch_shapes=[
            pltpu.VMEM((N_CTX, 2, 32, 4096), bf16),
            pltpu.VMEM((4, 1024, 512), bf16),
            pltpu.VMEM((N_CTX, 32, 512), bf16),
            pltpu.VMEM((N_CTX, 32, 512), bf16),
            pltpu.VMEM((N_CTX, 32, 512), f32),
            pltpu.VMEM((N_CTX, 32, 512), bf16),
            pltpu.VMEM((32, 8192), bf16),
            pltpu.SemaphoreType.DMA((2, 4)),
            pltpu.SemaphoreType.DMA((2, 4)),
            pltpu.SemaphoreType.DMA((2, 20)),
            pltpu.SemaphoreType.DMA((2, 32)),
            pltpu.SemaphoreType.DMA((4,)),
            pltpu.SemaphoreType.DMA((4,)),
            pltpu.SemaphoreType.DMA((N_CTX,)),
            pltpu.SemaphoreType.DMA((N_CTX,)),
            pltpu.SemaphoreType.DMA((3,)),
        ],
        compiler_params=pltpu.CompilerParams(
            collective_id=2, has_side_effects=True, vmem_limit_bytes=62 * MIB
        ),
        cost_estimate=pl.CostEstimate(
            flops=2 * 512 * 512 * 8192, bytes_accessed=20 * MIB, transcendentals=0
        ),
    )(attended, weight)

    paged_kv = pages.reshape(PAGE, PAGE, 2, D_HEAD)
    return (projected, paged_kv)


def solution(mesh):
    return jax.shard_map(
        local,
        mesh=mesh,
        in_specs=(
            P("ctx", "tp"),
            P("ctx", "tp"),
            P("ctx", "tp"),
            P("ctx", "tp"),
            P("ctx", "tp"),
            P(),
            P("ctx"),
            P("tp", "ctx"),
        ),
        out_specs=(P(("ctx", "tp"), None), P("ctx", None, None, "tp")),
        check_vma=False,
    )
```
